512 devices in a mesh: segment: 2 (over z_hi), group: 32 (over y, x, core), tensor: 8 (over z_lo).
Axes of the slice: x: 4, y: 4, z: 16 (z_hi: 2, z_lo: 8; z = z_hi * 8 + z_lo), core: 2. Of those that a mesh axis runs over, the one named last changes fastest.
Arguments:
- hidden: bfloat16 [24576, 8192], P(('segment', 'group'), 'tensor'), may hold values from -6 to 6
- prompt_queries: bfloat16 [24576, 8192], P(('segment', 'group'), 'tensor'), may hold values from -6 to 6
- prompt_key_values: bfloat16 [24576, 2048], P(('segment', 'group'), 'tensor'), may hold values from -6 to 6
- adapter_down_weight: bfloat16 [3, 8192, 128], P(None, 'tensor'), may hold values from -0.0625 to 0.0625
- adapter_up_weight: bfloat16 [3, 128, 2048], P(None, None, 'tensor'), may hold values from -0.5 to 0.5
- adapter_ranks: int32 [3], replicated, may hold values from 8 to 128, as said below
- tenant: int32 [64, 16], P(('segment', 'group')), may hold values from 0 to 2
- lengths: int32 [64, 16], replicated, may hold values from 1 to 32, 384 in all within a row
- owner: int32 [64, 16], replicated, may hold values from 0 to 31, as said below
- cached_key_values: bfloat16 [1024, 256, 2048], P(('segment', 'group'), 'tensor'), may hold values from -6 to 6
- draft_queries: bfloat16 [4096, 8192], P(('segment', 'group'), 'tensor'), may hold values from -6 to 6
- draft_key_values: bfloat16 [4096, 2048], P(('segment', 'group'), 'tensor'), may hold values from -6 to 6
Outputs:
- prompt_out: bfloat16 [24576, 8192], P(('segment', 'group'), 'tensor')
- decode_out: bfloat16 [4096, 8192], P(('segment', 'group'), 'tensor')
The draws below stay inside these ranges and needn't reach their ends.
Inputs may be any that keep to these rules, and one draw needn't show every extreme that they name: `owner`: each decode group receives exactly one request of each index i < 16 from the other section; one prefill group sends exactly 1 request to each of 16 decode groups and none to the others. `adapter_ranks`: powers of two.
All inputs are finite; a program needn't handle non-finite values.
Results may differ from the reference program's by a relative error of at most 0.0083.
Values may be sent and summed in bfloat16 or wider, within the bound.
A program may use at most 128 MiB of HBM per device.

```python
import math
import jax
import jax.numpy as jnp
import numpy as np
from jax import lax

MODEL_WIDTH = 8192
QH = 64
KEY_VALUE_HEADS = 8
HEAD_SIZE = 128
PADDED_RANK = 128
TENANT_ADAPTERS = 3
REQ = 16
PROMPT_TOKENS = 384
CTX = 256
SPEC = 4
CAP = 1
MAXLEN = 32
TOKENS = 24576
ALLREQ = 1024
N_SEGMENT = 2
N_GROUP = 32


def draw_owner(key, part):
    key = jax.random.fold_in(key, 11)
    blocks = []
    for section in range(N_SEGMENT):
        section_key = jax.random.fold_in(key, section)
        group_order = jax.random.permutation(jax.random.fold_in(section_key, 1), N_GROUP)
        distinct = jax.random.permutation(jax.random.fold_in(section_key, 2), N_GROUP)[:REQ // CAP]
        shifts = jax.random.permutation(jax.random.fold_in(section_key, 3), jnp.repeat(distinct, CAP))
        blocks.append((group_order[:, None] + shifts[None, :]) % N_GROUP)
    return jnp.concatenate(blocks, axis=0).astype(jnp.int32)


def draw_adapter_ranks(key, part):
    key = jax.random.fold_in(key, 12)
    top_power = PADDED_RANK.bit_length() - 1
    powers = jax.random.randint(key, (TENANT_ADAPTERS,), 3, top_power + 1)
    largest = jax.random.randint(jax.random.fold_in(key, 1), (), 0, TENANT_ADAPTERS)
    smallest = (largest + 1) % TENANT_ADAPTERS
    adapter_ids = jnp.arange(TENANT_ADAPTERS)
    powers = jnp.where(adapter_ids == largest, top_power, powers)
    powers = jnp.where(adapter_ids == smallest, 3, powers)
    return jnp.left_shift(jnp.int32(1), powers.astype(jnp.int32)).astype(jnp.int32)


def draw_prompt_queries(key, part):
    key = jax.random.fold_in(key, 21)
    values = jax.random.truncated_normal(key, -6.0, 6.0, (TOKENS, QH * HEAD_SIZE), jnp.float32)
    return values.astype(jnp.bfloat16)


def draw_prompt_key_values(key, part):
    key = jax.random.fold_in(key, 22)
    values = jax.random.truncated_normal(key, -6.0, 6.0, (TOKENS, KEY_VALUE_HEADS, 2, HEAD_SIZE), jnp.float32)
    return values.reshape(TOKENS, KEY_VALUE_HEADS * 2 * HEAD_SIZE).astype(jnp.bfloat16)


def draw_draft_queries(key, part):
    key = jax.random.fold_in(key, 23)
    values = jax.random.truncated_normal(key, -6.0, 6.0, (ALLREQ, SPEC, QH * HEAD_SIZE), jnp.float32)
    return values.reshape(ALLREQ * SPEC, QH * HEAD_SIZE).astype(jnp.bfloat16)


def draw_cached_key_values(key, part):
    key = jax.random.fold_in(key, 24)
    values = jax.random.truncated_normal(key, -6.0, 6.0, (ALLREQ, CTX, KEY_VALUE_HEADS, 2, HEAD_SIZE), jnp.float32)
    return values.reshape(ALLREQ, CTX, KEY_VALUE_HEADS * 2 * HEAD_SIZE).astype(jnp.bfloat16)


def plant(entries, rng, low, high):
    longest = entries.shape.index(max(entries.shape))
    spots = []
    for shift in (0, 1):
        where = [jax.random.randint(jax.random.fold_in(rng, axis), (), 0, length) for axis, length in enumerate(entries.shape)]
        where[longest] = (where[longest] + shift) % entries.shape[longest]
        spots.append(tuple(where))
    return entries.at[spots[0]].set(low).at[spots[1]].set(high)


def block_levels(own_key, extent, cuts, least, high):
    loudness, own = 1.0, jax.random.fold_in(own_key, 6)
    for dim, parts in cuts:
        draws = jnp.exp(jax.random.uniform(jax.random.fold_in(own, dim), (parts,), jnp.float32, least / len(cuts), high / len(cuts)))
        loudness = loudness * jnp.repeat(draws, extent[dim] // parts).reshape([-1 if axis == dim else 1 for axis in range(len(extent))])
    return loudness


def length_profile(amount, total, most, skew):
    portions = [(1 << 20) // math.isqrt(rank ** skew) + 1 for rank in range(2, amount + 1)]
    rest, given = total - most - (amount - 1), [1] * (amount - 1)
    while rest > 0:
        free = [i for i in range(amount - 1) if given[i] < most]
        whole, left = sum([portions[i] for i in free]), rest
        for i in free:
            extra = min(most - given[i], max(1, left * portions[i] // whole), rest)
            given[i] = given[i] + extra
            rest = rest - extra
    return np.array([most] + given)


def uneven(own_key, number_of, total, bound, skew):
    if number_of == 2:
        one = jax.random.randint(own_key, (), max(1, total - bound), min(bound, total - 1) + 1)
        return jnp.stack([one, total - one])
    tallies = jnp.asarray(length_profile(number_of, total, bound, skew), jnp.int32)
    twos = (number_of - 1) // 2
    giver, sink = tallies[1:1 + 2 * twos:2], tallies[2:2 + 2 * twos:2]
    room = jnp.minimum(giver - 1, bound - sink)
    shifted = jax.random.randint(jax.random.fold_in(own_key, 1), (twos,), 0, 1 << 20) % (room + 1)
    tallies = tallies.at[1:1 + 2 * twos:2].set(giver - shifted).at[2:2 + 2 * twos:2].set(sink + shifted)
    return tallies[jax.random.permutation(jax.random.fold_in(own_key, 2), number_of)]


def gaussian(stream_key, extent, spread, reach, pieces=(), held_as=jnp.bfloat16):
    drawn = jax.random.normal(stream_key, extent, jnp.float32) * spread
    if len(pieces) > 0:
        drawn = block_levels(stream_key, extent, pieces, -0.22, 0.18) * drawn
    return jnp.clip(drawn, min=-reach, max=reach).astype(held_as)


def setup_inputs(seed: int = 0) -> dict:
    splits = jax.random.split(jax.random.key(seed), 13)
    hidden = gaussian(splits[0], (TOKENS, MODEL_WIDTH), 1.0, 6.0, ((0, 64), (1, 8)))
    prompt_queries = draw_prompt_queries(jax.random.fold_in(splits[12], 71), 0)
    prompt_key_values = draw_prompt_key_values(jax.random.fold_in(splits[12], 71), 0)
    adapter_down_weight = gaussian(splits[3], (TENANT_ADAPTERS, MODEL_WIDTH, PADDED_RANK), MODEL_WIDTH ** -0.5, 0.0625, ((1, 8),))
    adapter_up_weight = gaussian(splits[4], (TENANT_ADAPTERS, PADDED_RANK, KEY_VALUE_HEADS * 2 * HEAD_SIZE), PADDED_RANK ** -0.5, 0.5, ((2, 8),))
    adapter_ranks = draw_adapter_ranks(jax.random.fold_in(splits[12], 71), 0)
    tenant = plant(jax.random.randint(splits[6], (N_SEGMENT * N_GROUP, REQ), 0, TENANT_ADAPTERS), jax.random.fold_in(splits[6], 1), 0, TENANT_ADAPTERS - 1).astype(jnp.int32)
    lengths = jax.vmap(lambda own: uneven(own, REQ, PROMPT_TOKENS, MAXLEN, 2))(jax.random.split(splits[7], (N_SEGMENT * N_GROUP))).reshape((N_SEGMENT * N_GROUP, REQ)).astype(jnp.int32)
    owner = draw_owner(jax.random.fold_in(splits[12], 71), 0)
    cached_key_values = draw_cached_key_values(jax.random.fold_in(splits[12], 71), 0)
    draft_queries = draw_draft_queries(jax.random.fold_in(splits[12], 71), 0)
    draft_key_values = gaussian(splits[11], (ALLREQ * SPEC, KEY_VALUE_HEADS * 2 * HEAD_SIZE), 1.0, 6.0, ((0, 64), (1, 8)))
    return {"hidden": hidden, "prompt_queries": prompt_queries, "prompt_key_values": prompt_key_values, "adapter_down_weight": adapter_down_weight, "adapter_up_weight": adapter_up_weight, "adapter_ranks": adapter_ranks, "tenant": tenant, "lengths": lengths, "owner": owner, "cached_key_values": cached_key_values, "draft_queries": draft_queries, "draft_key_values": draft_key_values}


negative = -1e+30

def token_requests(row_lengths, count):
    req_ends = jnp.cumsum(row_lengths)
    positions = jnp.arange(count, dtype=jnp.int32)
    return lax.optimization_barrier(jnp.sum((positions[:, None] >= req_ends[None, :]).astype(jnp.int32), axis=1))

def reference(hidden, prompt_queries, prompt_key_values, adapter_down_weight, adapter_up_weight, adapter_ranks, tenant, lengths, owner, cached_key_values, draft_queries, draft_key_values):
    score_scale = HEAD_SIZE ** (-0.5)
    sections = N_SEGMENT * N_GROUP
    feature_width = KEY_VALUE_HEADS * 2 * HEAD_SIZE

    def prefill(group_items):
        group_hidden_rows, group_q, group_key_values, group_lengths, group_tenant = group_items
        request = token_requests(group_lengths, PROMPT_TOKENS)
        tenant_adapter = group_tenant[request]
        rank_tok = adapter_ranks[tenant_adapter]
        reduced_rows = jnp.zeros((PROMPT_TOKENS, PADDED_RANK), jnp.float32)
        for adapter_index in range(TENANT_ADAPTERS):
            partial_value_sum = jnp.dot(group_hidden_rows, adapter_down_weight[adapter_index], preferred_element_type=jnp.float32)
            reduced_rows = jnp.where((tenant_adapter == adapter_index)[:, None], partial_value_sum, reduced_rows)
        columns = jnp.arange(PADDED_RANK, dtype=jnp.int32)
        reduced_rows = jnp.where(columns[None, :] < rank_tok[:, None], reduced_rows, 0.0).astype(jnp.bfloat16)
        adapter_delta = jnp.zeros((PROMPT_TOKENS, feature_width), jnp.float32)
        for adapter_index in range(TENANT_ADAPTERS):
            expanded_rows = jnp.dot(reduced_rows, adapter_up_weight[adapter_index], preferred_element_type=jnp.float32)
            adapter_delta = jnp.where((tenant_adapter == adapter_index)[:, None], expanded_rows, adapter_delta)
        lowrank_factor = 8.0 / jnp.sqrt(rank_tok.astype(jnp.float32))
        key_value_rows = (group_key_values.astype(jnp.float32) + lowrank_factor[:, None] * adapter_delta).astype(jnp.bfloat16)
        kv_split = key_value_rows.reshape(PROMPT_TOKENS, KEY_VALUE_HEADS, 2, HEAD_SIZE).astype(jnp.float32)
        queries = group_q.reshape(PROMPT_TOKENS, KEY_VALUE_HEADS, QH // KEY_VALUE_HEADS, HEAD_SIZE).astype(jnp.float32)
        scores = jnp.einsum('pjgd,kjd->jgpk', queries, kv_split[:, :, 0], precision=lax.Precision.HIGHEST) * score_scale
        positions = jnp.arange(PROMPT_TOKENS, dtype=jnp.int32)
        allowed = (request[:, None] == request[None, :]) & (positions[None, :] <= positions[:, None])
        scores = jnp.where(allowed, scores, negative)
        row_max = lax.optimization_barrier(jnp.max(scores, axis=-1, keepdims=True))
        exp_scores = jnp.exp(scores - row_max)
        weights = (exp_scores / lax.optimization_barrier(jnp.sum(exp_scores, axis=-1, keepdims=True))).astype(jnp.bfloat16)
        attended = jnp.einsum('jgpk,kjd->pjgd', weights.astype(jnp.float32), kv_split[:, :, 1], precision=lax.Precision.HIGHEST)
        return (attended.reshape(PROMPT_TOKENS, QH * HEAD_SIZE).astype(jnp.bfloat16), key_value_rows)
    prompt_out, keyvals_all = lax.map(prefill, (hidden.reshape(sections, PROMPT_TOKENS, MODEL_WIDTH), prompt_queries.reshape(sections, PROMPT_TOKENS, QH * HEAD_SIZE), prompt_key_values.reshape(sections, PROMPT_TOKENS, feature_width), lengths, tenant))
    flat_kv = keyvals_all.reshape(sections * PROMPT_TOKENS, feature_width)

    def decode(group_items):
        group_index, group_cache, group_q, group_key_values = group_items
        segment_here = group_index // N_GROUP
        group_here = group_index % N_GROUP
        other_rows = (1 - segment_here) * N_GROUP
        src_owner = lax.dynamic_slice_in_dim(owner, other_rows, N_GROUP, 0)
        src_lengths = lax.dynamic_slice_in_dim(lengths, other_rows, N_GROUP, 0)
        is_mine = src_owner == group_here
        source = lax.optimization_barrier(jnp.sum(jnp.where(is_mine, jnp.arange(N_GROUP, dtype=jnp.int32)[:, None], 0), axis=0))
        src_starts = jnp.cumsum(src_lengths, axis=1) - src_lengths
        slot_ids = jnp.arange(REQ, dtype=jnp.int32)
        src_start = src_starts[source, slot_ids]
        src_length = src_lengths[source, slot_ids]
        row_base = (other_rows + source) * PROMPT_TOKENS + src_start
        offsets = jnp.arange(MAXLEN, dtype=jnp.int32)
        live_new = offsets[None, :] < src_length[:, None]
        row_index = jnp.where(live_new, row_base[:, None] + offsets[None, :], 0)
        handed = flat_kv[row_index]
        key_vals = jnp.concatenate([group_cache, handed, group_key_values.reshape(REQ, SPEC, feature_width)], axis=1)
        key_vals = key_vals.astype(jnp.float32).reshape(REQ, CTX + MAXLEN + SPEC, KEY_VALUE_HEADS, 2, HEAD_SIZE)
        draft_ids = jnp.arange(SPEC, dtype=jnp.int32)
        own_live = draft_ids[None, :] <= draft_ids[:, None]
        is_live = jnp.concatenate([jnp.ones((REQ, SPEC, CTX), bool), jnp.broadcast_to(live_new[:, None, :], (REQ, SPEC, MAXLEN)), jnp.broadcast_to(own_live[None], (REQ, SPEC, SPEC))], axis=2)
        queries = group_q.reshape(REQ, SPEC, KEY_VALUE_HEADS, QH // KEY_VALUE_HEADS, HEAD_SIZE).astype(jnp.float32)
        scores = jnp.einsum('rsjgd,rljd->rsjgl', queries, key_vals[:, :, :, 0], precision=lax.Precision.HIGHEST) * score_scale
        scores = jnp.where(is_live[:, :, None, None, :], scores, negative)
        row_max = lax.optimization_barrier(jnp.max(scores, axis=-1, keepdims=True))
        exp_scores = jnp.exp(scores - row_max)
        weights = exp_scores / lax.optimization_barrier(jnp.sum(exp_scores, axis=-1, keepdims=True))
        attended = jnp.einsum('rsjgl,rljd->rsjgd', weights, key_vals[:, :, :, 1], precision=lax.Precision.HIGHEST)
        return attended.reshape(REQ * SPEC, QH * HEAD_SIZE).astype(jnp.bfloat16)
    decode_out = lax.map(decode, (jnp.arange(sections, dtype=jnp.int32), cached_key_values.reshape(sections, REQ, CTX, feature_width), draft_queries.reshape(sections, REQ * SPEC, QH * HEAD_SIZE), draft_key_values.reshape(sections, REQ * SPEC, feature_width)))
    return (prompt_out.reshape(TOKENS, QH * HEAD_SIZE), decode_out.reshape(ALLREQ * SPEC, QH * HEAD_SIZE))
```

```python
import jax
import jax.numpy as jnp
from jax import lax
from jax.experimental import pallas as pl
from jax.experimental.pallas import tpu as pltpu
from jax.sharding import PartitionSpec as P

HEAD = 128
GQA = 8
SPEC = 4
MAXLEN = 32
REQ = 16
NT = 8
NG = 32
TOK = 384
BLK = TOK // NT
ADAPTERS = 3
PARTS = 4
QROWS = REQ * SPEC // PARTS
KVW = 2 * HEAD
MSG = HEAD + 16
TILE = 96
SCALE = HEAD**-0.5
NEG = -1e30
MESH = pl.DeviceIdType.MESH
F32 = jnp.float32
BF16 = jnp.bfloat16


def nt_dot(a, b):
    return lax.dot_general(a, b, (((1,), (1,)), ((), ())), preferred_element_type=F32)


def tn_dot(a, b):
    return lax.dot_general(a, b, (((0,), (0,)), ((), ())), preferred_element_type=F32)


def iota(shape, dim):
    return lax.broadcasted_iota(jnp.int32, shape, dim)


def merge(a, b):
    num_a, m_a, l_a = a
    num_b, m_b, l_b = b
    m = jnp.maximum(m_a, m_b)
    f_a = jnp.exp(m_a - m)
    f_b = jnp.exp(m_b - m)
    return num_a * f_a + num_b * f_b, m, l_a * f_a + l_b * f_b


def partial_attention(keys, values, queries, mask):
    s = nt_dot(keys, queries) * SCALE
    s = jnp.where(mask, s, NEG)
    m = jnp.max(s, axis=0, keepdims=True).astype(BF16).astype(F32)
    p = jnp.where(mask, jnp.exp(s - m), 0.0)
    total = jnp.sum(p, axis=0, keepdims=True)
    num = tn_dot(values, p.astype(BF16))
    return num, m, total


def request_rows(lens, owner, row):
    lane = iota((1, 128), 1)
    start_row = jnp.full((1, 128), 1 << 20, jnp.int32)
    end_row = jnp.full((1, 128), 1 << 20, jnp.int32)
    owner_row = jnp.full((1, 128), -1, jnp.int32)
    at = jnp.int32(0)
    for i in range(REQ):
        n = lens[row, i]
        start_row = jnp.where(lane == i, at, start_row)
        at = at + n
        end_row = jnp.where(lane == i, at, end_row)
        owner_row = jnp.where(lane == i, owner[row, i], owner_row)
    return start_row, end_row, owner_row


def token_columns(start_row, end_row, tenant_row, ranks):
    pos = iota((TOK, 128), 0)
    hit = (pos >= start_row) & (pos < end_row)
    start = jnp.sum(jnp.where(hit, start_row.astype(F32), 0.0), axis=1, keepdims=True)
    adapter = jnp.sum(jnp.where(hit, tenant_row.astype(F32), 0.0), axis=1, keepdims=True)
    rank = jnp.zeros((TOK, 1), F32)
    for a in range(ADAPTERS):
        rank = jnp.where(adapter == float(a), ranks[a].astype(F32), rank)
    return start, adapter, rank


def kernel(
    hid, pq, pkv, down, up, ranks, tenant, lens, owner, cache, dq, dkv,
    pout, dout,
    hid_v, pq_v, pkv_v, down_v, up_v, cache_v, dkv_v, qall,
    own_num, own_st, sendb, recv_r, recv_l,
    rs_send, rs_recv, sh_own, sh_oth, pkv_o, ten_own, ten_oth,
    kv_own, packed, handed, acc, acc_st, pout_v, dout_v, slot_tab,
    lsem, qs, qr, ps, pr, rss, rsr, ags, agr, xs, xr, hs, hr, osem,
):
    s = lax.axis_index("segment")
    g = lax.axis_index("group")
    t = lax.axis_index("tensor")

    loads = []
    for k, (src, dst) in enumerate(
        [(dq, qall.at[t]), (hid, hid_v), (down, down_v), (pkv, pkv_v), (up, up_v),
         (cache, cache_v), (dkv, dkv_v), (pq, pq_v)]
    ):
        c = pltpu.make_async_copy(src, dst, lsem.at[k])
        c.start()
        loads.append(c)
    ld_q, ld_hid, ld_down, ld_pkv, ld_up, ld_cache, ld_dkv, ld_pq = loads

    barrier = pltpu.get_barrier_semaphore()

    def greet_tensor(k, _):
        pl.semaphore_signal(barrier, inc=1, device_id={"tensor": lax.rem(t + k, NT)}, device_id_type=MESH)
        return _

    def greet_cross(k, _):
        pl.semaphore_signal(
            barrier, inc=1, device_id={"segment": 1 - s, "tensor": lax.rem(t + k, NT)}, device_id_type=MESH
        )
        return _

    def greet_group(k, _):
        pl.semaphore_signal(barrier, inc=1, device_id={"group": lax.rem(g + k, NG)}, device_id_type=MESH)
        return _

    lax.fori_loop(1, NT, greet_tensor, 0)
    lax.fori_loop(0, NT, greet_cross, 0)
    lax.fori_loop(1, NG, greet_group, 0)

    here = s * NG + g
    there = (1 - s) * NG + g
    lane = iota((8, 128), 1)
    tenants = jnp.zeros((8, 128), jnp.int32)
    for i in range(REQ):
        tenants = jnp.where(lane == i, tenant[0, i], tenants)
    ten_own[...] = tenants
    start_row, end_row, _ = request_rows(lens, owner, here)
    start, adapter, rank = token_columns(start_row, end_row, tenants[0:1], ranks)

    pl.semaphore_wait(barrier, (NT - 1) + NT + (NG - 1))

    def q_copy(j, c, side):
        rows = pl.ds(c * QROWS, QROWS)
        return pltpu.make_async_remote_copy(
            src_ref=qall.at[j, rows],
            dst_ref=qall.at[j, rows],
            send_sem=qs.at[side, j, c],
            recv_sem=qr.at[j, c],
            device_id={"tensor": lax.rem(t + (1 if side == 0 else NT - 1), NT)},
            device_id_type=MESH,
        )

    def p_copy(j, c, side):
        return pltpu.make_async_remote_copy(
            src_ref=sendb.at[j, c],
            dst_ref=(recv_r if side == 0 else recv_l).at[j, c],
            send_sem=ps.at[side, j, c],
            recv_sem=pr.at[side, j, c],
            device_id={"tensor": lax.rem(t + (1 if side == 0 else NT - 1), NT)},
            device_id_type=MESH,
        )

    def rs_copy(k, src):
        return pltpu.make_async_remote_copy(
            src_ref=rs_send.at[k],
            dst_ref=rs_recv.at[src],
            send_sem=rss.at[k],
            recv_sem=rsr.at[src],
            device_id={"tensor": k},
            device_id_type=MESH,
        )

    def ag_copy(k, src):
        return pltpu.make_async_remote_copy(
            src_ref=sh_own.at[src],
            dst_ref=sh_own.at[src],
            send_sem=ags.at[0, k],
            recv_sem=agr.at[0, src],
            device_id={"tensor": k},
            device_id_type=MESH,
        )

    def cross_copy(k, src):
        return pltpu.make_async_remote_copy(
            src_ref=sh_own.at[src],
            dst_ref=sh_oth.at[src],
            send_sem=ags.at[1, k],
            recv_sem=agr.at[1, src],
            device_id={"segment": 1 - s, "tensor": k},
            device_id_type=MESH,
        )

    def base_copy():
        return pltpu.make_async_remote_copy(
            src_ref=pkv_v,
            dst_ref=pkv_o,
            send_sem=xs.at[0],
            recv_sem=xr.at[0],
            device_id={"segment": 1 - s},
            device_id_type=MESH,
        )

    def tenant_copy():
        return pltpu.make_async_remote_copy(
            src_ref=ten_own,
            dst_ref=ten_oth,
            send_sem=xs.at[1],
            recv_sem=xr.at[1],
            device_id={"segment": 1 - s},
            device_id_type=MESH,
        )

    def hand_copy(d, src):
        return pltpu.make_async_remote_copy(
            src_ref=packed.at[d],
            dst_ref=handed.at[src],
            send_sem=hs.at[d],
            recv_sem=hr.at[src],
            device_id={"group": d},
            device_id_type=MESH,
        )

    ld_q.wait()

    @pl.when(t < NT - 1)
    def _():
        for c in range(PARTS):
            q_copy(t, c, 0).start()

    @pl.when(t > 0)
    def _():
        for c in range(PARTS):
            q_copy(t, c, 1).start()

    ld_pkv.wait()
    tenant_copy().start()
    base_copy().start()

    ld_hid.wait()
    ld_down.wait()
    col = iota((TOK, HEAD), 1)
    selected = jnp.zeros((TOK, HEAD), F32)
    for a in range(ADAPTERS):
        part = jnp.dot(hid_v[...], down_v[a], preferred_element_type=F32)
        selected = jnp.where(adapter == float(a), part, selected)
    selected = jnp.where(col.astype(F32) < rank, selected, 0.0)
    rs_send[...] = selected.reshape(NT, BLK, HEAD)

    def rs_start(k, _):
        rs_copy(lax.rem(t + k, NT), t).start()
        return _

    lax.fori_loop(1, NT, rs_start, 0)

    def reduce_and_share():
        def add(k, total):
            src = lax.rem(t + k, NT)
            rs_copy(src, src).wait_recv()
            return total + rs_recv[src]

        total = lax.fori_loop(1, NT, add, rs_send[t])
        sh_own[t] = total.astype(BF16)

        def share(k, _):
            to = lax.rem(t + k, NT)
            ag_copy(to, t).start()
            cross_copy(to, t).start()
            return _

        lax.fori_loop(1, NT, share, 0)
        cross_copy(t, t).start()

    def lora_rows(shrunk, base, adapter_col, rank_col):
        delta = jnp.zeros((TOK, KVW), F32)
        for a in range(ADAPTERS):
            part = jnp.dot(shrunk, up_v[a], preferred_element_type=F32)
            delta = jnp.where(adapter_col == float(a), part, delta)
        return (base.astype(F32) + (8.0 / jnp.sqrt(rank_col)) * delta).astype(BF16)

    def hand_over():
        start_p, end_p, owner_p = request_rows(lens, owner, there)
        group_of = iota((NG * MAXLEN, 128), 0) // MAXLEN
        code = (start_p * 64 + (end_p - start_p)).astype(F32)
        found = jnp.sum(jnp.where(group_of == owner_p, code, 0.0), axis=1, keepdims=True)
        found = found.astype(jnp.int32)
        offset = iota((NG * MAXLEN, 1), 0) % MAXLEN
        source = jnp.where(offset < found % 64, found // 64 + offset, -1)
        pick = (iota((NG * MAXLEN, TOK), 1) == source).astype(F32).astype(BF16)
        tenant_copy().wait_recv()
        _, adapter_p, rank_p = token_columns(start_p, end_p, ten_oth[0:1, :], ranks)
        base_copy().wait_recv()
        ld_up.wait()

        def arrive(k, _):
            src = lax.rem(t + k, NT)
            cross_copy(src, src).wait_recv()
            return _

        lax.fori_loop(0, NT, arrive, 0)
        rows = lora_rows(sh_oth[...].reshape(TOK, HEAD), pkv_o[...], adapter_p, rank_p)
        moved = jnp.dot(pick, rows, preferred_element_type=F32).astype(BF16)
        packed[...] = moved.reshape(NG, MAXLEN, KVW)

        def send(k, _):
            d = lax.rem(g + k, NG)
            hand_copy(d, g).start()
            return _

        lax.fori_loop(1, NG, send, 0)
        handed[g] = packed[g]

    def own_rows():
        def arrive(k, _):
            src = lax.rem(t + k, NT)
            ag_copy(src, src).wait_recv()
            return _

        lax.fori_loop(1, NT, arrive, 0)
        kv_own[...] = lora_rows(sh_own[...].reshape(TOK, HEAD), pkv_v[...], adapter, rank)

    def prompt_tile(n):
        low = max(n * TILE - 32, 0)
        keys = kv_own[low:low + 128, 0:HEAD]
        values = kv_own[low:low + 128, HEAD:KVW]
        q_pos = iota((TILE, 128), 0) + n * TILE
        k_pos = iota((TILE, 128), 1) + low
        first = start[n * TILE:(n + 1) * TILE].astype(jnp.int32)
        mask = (k_pos >= first) & (k_pos <= q_pos)
        for h in range(GQA):
            q = pq_v[n * TILE:(n + 1) * TILE, h * HEAD:(h + 1) * HEAD]
            sc = jnp.where(mask, nt_dot(q, keys) * SCALE, NEG)
            e = jnp.exp(sc - jnp.max(sc, axis=1, keepdims=True))
            w = (e / jnp.sum(e, axis=1, keepdims=True)).astype(BF16)
            o = jnp.dot(w, values, preferred_element_type=F32)
            pout_v[n * TILE:(n + 1) * TILE, h * HEAD:(h + 1) * HEAD] = o.astype(BF16)

    def out_copy(n):
        rows = pl.ds(n * TILE, TILE)
        return pltpu.make_async_copy(pout_v.at[rows], pout.at[rows], osem.at[n])

    q_lane = iota((128, 128), 1) % QROWS
    k_row = iota((128, 128), 0)
    same_slot = (k_row // MAXLEN) == (q_lane // SPEC)

    def stacked(j, part):
        rows = slice(part * QROWS, (part + 1) * QROWS)
        return jnp.concatenate([qall[j, rows, h * HEAD:(h + 1) * HEAD] for h in range(GQA)], axis=0)

    def cached_partial(j, part):
        at = pl.multiple_of(j * KVW, KVW)
        slots = slice(part * 4, part * 4 + 4)
        keys = cache_v[slots, :, pl.ds(at, HEAD)].reshape(128, HEAD)
        values = cache_v[slots, :, pl.ds(at + HEAD, HEAD)].reshape(128, HEAD)
        return partial_attention(keys, values, stacked(j, part), same_slot)

    def put_message(j, part, num, m, total):
        high = total.astype(BF16)
        low = (total - high.astype(F32)).astype(BF16)
        sendb[j, part, 0:HEAD, :] = num.astype(BF16)
        row = iota((16, 128), 0)
        stats = jnp.where(row == 0, m, jnp.where(row == 1, high.astype(F32), low.astype(F32)))
        sendb[j, part, HEAD:MSG, :] = stats.astype(BF16)

    def get_message(buf, j, part):
        stats = buf[j, part, HEAD:MSG, :].astype(F32)
        return buf[j, part, 0:HEAD, :].astype(F32), stats[0:1], stats[1:2] + stats[2:3]

    def own_partial(j, part):
        return own_num[j, part], own_st[j, part, 0:1, :], own_st[j, part, 1:2, :]

    def attend_head(j):
        for part in range(PARTS):
            num, m, total = cached_partial(j, part)
            own_num[j, part] = num
            own_st[j, part, 0:1, :] = m
            own_st[j, part, 1:2, :] = total

    def first_link(j, side):
        for part in range(PARTS):
            put_message(j, part, *own_partial(j, part))
            p_copy(j, part, side).start()

    def next_link(j, side):
        buf = recv_r if side == 0 else recv_l
        for part in range(PARTS):
            p_copy(j, part, side).wait_recv()
            put_message(j, part, *merge(get_message(buf, j, part), own_partial(j, part)))
            p_copy(j, part, side).start()

    def put_acc(part, num, m, total):
        acc[part] = num
        acc_st[part, 0:1, :] = m
        acc_st[part, 1:2, :] = total

    def get_acc(part):
        return acc[part], acc_st[part, 0:1, :], acc_st[part, 1:2, :]

    def own_and_drafts():
        k_draft = iota((QROWS, 128), 0)
        q_draft = iota((QROWS, 128), 1) % QROWS
        mask = (k_draft // SPEC == q_draft // SPEC) & (k_draft % SPEC <= q_draft % SPEC)
        for part in range(PARTS):
            rows = slice(part * QROWS, (part + 1) * QROWS)
            draft = partial_attention(
                dkv_v[rows, 0:HEAD], dkv_v[rows, HEAD:KVW], stacked(t, part), mask
            )
            put_acc(part, *merge(cached_partial(t, part), draft))

    def find_slots():
        other = (1 - s) * NG
        for i in range(REQ):
            def look(k, src):
                return jnp.where(owner[other + k, i] == g, k, src)

            src = lax.fori_loop(0, NG, look, jnp.int32(0), unroll=True)
            slot_tab[0, i] = src
            slot_tab[1, i] = lens[other + src, i]

    def handed_attention():
        def arrive(k, _):
            src = lax.rem(g + k, NG)
            hand_copy(src, src).wait_recv()
            return _

        lax.fori_loop(1, NG, arrive, 0)
        for part in range(PARTS):
            keys, values = [], []
            limit = jnp.zeros((128, 128), jnp.int32)
            for u in range(4):
                i = part * 4 + u
                block = handed[slot_tab[0, i]]
                keys.append(block[:, 0:HEAD])
                values.append(block[:, HEAD:KVW])
                limit = jnp.where(k_row // MAXLEN == u, slot_tab[1, i], limit)
            mask = same_slot & (k_row % MAXLEN < limit)
            found = partial_attention(
                jnp.concatenate(keys, axis=0), jnp.concatenate(values, axis=0), stacked(t, part), mask
            )
            put_acc(part, *merge(get_acc(part), found))

    def finish(side):
        buf = recv_r if side == 0 else recv_l
        for part in range(PARTS):
            p_copy(t, part, side).wait_recv()
            put_acc(part, *merge(get_acc(part), get_message(buf, t, part)))

    def step(tau, carry):
        from_right = t + tau
        from_left = t - tau

        @pl.when(from_right < NT)
        def _():
            for c in range(PARTS):
                q_copy(from_right, c, 1).wait_recv()

                @pl.when(t > 0)
                def _():
                    q_copy(from_right, c, 1).start()

        @pl.when(from_left >= 0)
        def _():
            for c in range(PARTS):
                q_copy(from_left, c, 0).wait_recv()

                @pl.when(t < NT - 1)
                def _():
                    q_copy(from_left, c, 0).start()

        @pl.when(tau == 1)
        def _():
            reduce_and_share()
            ld_cache.wait()

        @pl.when(from_right < NT)
        def _():
            attend_head(from_right)

            @pl.when(t == 0)
            def _():
                first_link(from_right, 0)

        @pl.when(from_left >= 0)
        def _():
            attend_head(from_left)

            @pl.when(t == NT - 1)
            def _():
                first_link(from_left, 1)

        to_right = tau - t

        @pl.when((t >= 1) & (to_right > t) & (to_right < NT))
        def _():
            next_link(to_right, 0)

        to_left = 2 * (NT - 1) - t - tau

        @pl.when((t <= NT - 2) & (to_left < t) & (to_left >= 0))
        def _():
            next_link(to_left, 1)

        @pl.when(tau == 2)
        def _():
            hand_over()

        @pl.when(tau == 3)
        def _():
            own_rows()
            ld_pq.wait()
            ld_dkv.wait()

        for n in range(TOK // TILE):
            @pl.when(tau == 4 + n)
            def _():
                prompt_tile(n)
                out_copy(n).start()

        @pl.when(tau == 8)
        def _():
            own_and_drafts()
            find_slots()

        @pl.when(tau == 9)
        def _():
            handed_attention()

        return carry

    lax.fori_loop(1, 2 * NT - 1, step, 0)

    @pl.when(t > 0)
    def _():
        finish(0)

    @pl.when(t < NT - 1)
    def _():
        finish(1)

    for part in range(PARTS):
        num, _, total = get_acc(part)
        out = jnp.transpose(num / total)
        for h in range(GQA):
            dout_v[part * QROWS:(part + 1) * QROWS, h * HEAD:(h + 1) * HEAD] = out[
                h * QROWS:(h + 1) * QROWS
            ].astype(BF16)
    last = pltpu.make_async_copy(dout_v, dout, osem.at[TOK // TILE])
    last.start()

    for side in range(2):
        edge = (t < NT - 1) if side == 0 else (t > 0)

        @pl.when(edge)
        def _(side=side):
            def each(j, carry):
                @pl.when((j <= t) if side == 0 else (j >= t))
                def _():
                    for c in range(PARTS):
                        q_copy(j, c, side).wait_send()

                @pl.when((j > t) if side == 0 else (j < t))
                def _():
                    for c in range(PARTS):
                        p_copy(j, c, side).wait_send()

                return carry

            lax.fori_loop(0, NT, each, 0)

    def left_tensor(k, _):
        to = lax.rem(t + k, NT)
        rs_copy(to, t).wait_send()
        ag_copy(to, t).wait_send()
        cross_copy(to, t).wait_send()
        return _

    lax.fori_loop(1, NT, left_tensor, 0)
    cross_copy(t, t).wait_send()
    base_copy().wait_send()
    tenant_copy().wait_send()

    def left_group(k, _):
        hand_copy(lax.rem(g + k, NG), g).wait_send()
        return _

    lax.fori_loop(1, NG, left_group, 0)
    for n in range(TOK // TILE):
        out_copy(n).wait()
    last.wait()


def body(*args):
    any_space = pl.BlockSpec(memory_space=pl.ANY)
    smem = pl.BlockSpec(memory_space=pltpu.SMEM)
    dma = pltpu.SemaphoreType.DMA
    return pl.pallas_call(
        kernel,
        out_shape=(
            jax.ShapeDtypeStruct((TOK, GQA * HEAD), BF16),
            jax.ShapeDtypeStruct((REQ * SPEC, GQA * HEAD), BF16),
        ),
        in_specs=[any_space] * 5 + [smem] * 4 + [any_space] * 3,
        out_specs=(any_space, any_space),
        scratch_shapes=[
            pltpu.VMEM((TOK, NT * HEAD), BF16),
            pltpu.VMEM((TOK, GQA * HEAD), BF16),
            pltpu.VMEM((TOK, KVW), BF16),
            pltpu.VMEM((ADAPTERS, NT * HEAD, HEAD), BF16),
            pltpu.VMEM((ADAPTERS, HEAD, KVW), BF16),
            pltpu.VMEM((REQ, 32, NT * KVW), BF16),
            pltpu.VMEM((REQ * SPEC, KVW), BF16),
            pltpu.VMEM((NT, REQ * SPEC, GQA * HEAD), BF16),
            pltpu.VMEM((NT, PARTS, HEAD, 128), F32),
            pltpu.VMEM((NT, PARTS, 8, 128), F32),
            pltpu.VMEM((NT, PARTS, MSG, 128), BF16),
            pltpu.VMEM((NT, PARTS, MSG, 128), BF16),
            pltpu.VMEM((NT, PARTS, MSG, 128), BF16),
            pltpu.VMEM((NT, BLK, HEAD), F32),
            pltpu.VMEM((NT, BLK, HEAD), F32),
            pltpu.VMEM((NT, BLK, HEAD), BF16),
            pltpu.VMEM((NT, BLK, HEAD), BF16),
            pltpu.VMEM((TOK, KVW), BF16),
            pltpu.VMEM((8, 128), jnp.int32),
            pltpu.VMEM((8, 128), jnp.int32),
            pltpu.VMEM((TOK, KVW), BF16),
            pltpu.VMEM((NG, MAXLEN, KVW), BF16),
            pltpu.VMEM((NG, MAXLEN, KVW), BF16),
            pltpu.VMEM((PARTS, HEAD, 128), F32),
            pltpu.VMEM((PARTS, 8, 128), F32),
            pltpu.VMEM((TOK, GQA * HEAD), BF16),
            pltpu.VMEM((REQ * SPEC, GQA * HEAD), BF16),
            pltpu.SMEM((2, REQ), jnp.int32),
            dma((8,)),
            dma((2, NT, PARTS)),
            dma((NT, PARTS)),
            dma((2, NT, PARTS)),
            dma((2, NT, PARTS)),
            dma((NT,)),
            dma((NT,)),
            dma((2, NT)),
            dma((2, NT)),
            dma((2,)),
            dma((2,)),
            dma((NG,)),
            dma((NG,)),
            dma((TOK // TILE + 1,)),
        ],
        compiler_params=pltpu.CompilerParams(
            collective_id=0, has_side_effects=True, vmem_limit_bytes=40 << 20
        ),
    )(*args)


def solution(mesh):
    rows = ("segment", "group")
    return jax.shard_map(
        body,
        mesh=mesh,
        in_specs=(
            P(rows, "tensor"),
            P(rows, "tensor"),
            P(rows, "tensor"),
            P(None, "tensor", None),
            P(None, None, "tensor"),
            P(),
            P(rows, None),
            P(),
            P(),
            P(rows, "tensor", None),
            P(rows, "tensor"),
            P(rows, "tensor"),
        ),
        out_specs=(P(rows, "tensor"), P(rows, "tensor")),
        check_vma=False,
    )
```

```python
import jax
import jax.numpy as jnp
from jax import lax
from jax.experimental import pallas as pl
from jax.experimental.pallas import tpu as pltpu
from jax.sharding import PartitionSpec as P

HEAD = 128
GQA = 8
SPEC = 4
MAXLEN = 32
REQ = 16
NT = 8
NG = 32
TOK = 384
BLK = TOK // NT
ADAPTERS = 3
PARTS = 4
QROWS = REQ * SPEC // PARTS
KVW = 2 * HEAD
STATS = 16
MSG = STATS + PARTS * HEAD
TILE = 96
SCALE = HEAD**-0.5
SHARE_AT = 3
OWN_AT = 5
HAND_AT = (9, 10)
TILE_AT = (6, 7, 8, 9)
HANDED_AT = 12
NEG = -1e30
MESH = pl.DeviceIdType.MESH
F32 = jnp.float32
BF16 = jnp.bfloat16


def nt_dot(a, b):
    return lax.dot_general(a, b, (((1,), (1,)), ((), ())), preferred_element_type=F32)


def tn_dot(a, b):
    return lax.dot_general(a, b, (((0,), (0,)), ((), ())), preferred_element_type=F32)


def iota(shape, dim):
    return lax.broadcasted_iota(jnp.int32, shape, dim)


def merge(a, b):
    num_a, m_a, l_a = a
    num_b, m_b, l_b = b
    m = jnp.maximum(m_a, m_b)
    f_a = jnp.exp(m_a - m)
    f_b = jnp.exp(m_b - m)
    return num_a * f_a + num_b * f_b, m, l_a * f_a + l_b * f_b


def partial_attention(keys, values, queries, mask):
    s = nt_dot(keys, queries) * SCALE
    s = jnp.where(mask, s, NEG)
    m = jnp.max(s, axis=0, keepdims=True).astype(BF16).astype(F32)
    p = jnp.where(mask, jnp.exp(s - m), 0.0)
    total = jnp.sum(p, axis=0, keepdims=True)
    num = tn_dot(values, p.astype(BF16))
    return num, m, total


def request_rows(lens, owner, row):
    lane = iota((1, 128), 1)
    start_row = jnp.full((1, 128), 1 << 20, jnp.int32)
    end_row = jnp.full((1, 128), 1 << 20, jnp.int32)
    owner_row = jnp.full((1, 128), -1, jnp.int32)
    at = jnp.int32(0)
    for i in range(REQ):
        n = lens[i, row]
        start_row = jnp.where(lane == i, at, start_row)
        at = at + n
        end_row = jnp.where(lane == i, at, end_row)
        owner_row = jnp.where(lane == i, owner[i, row], owner_row)
    return start_row, end_row, owner_row


def token_columns(start_row, end_row, tenant_row, ranks):
    pos = iota((TOK, 128), 0)
    hit = (pos >= start_row) & (pos < end_row)
    start = jnp.sum(jnp.where(hit, start_row.astype(F32), 0.0), axis=1, keepdims=True)
    adapter = jnp.sum(jnp.where(hit, tenant_row.astype(F32), 0.0), axis=1, keepdims=True)
    rank = jnp.zeros((TOK, 1), F32)
    for a in range(ADAPTERS):
        rank = jnp.where(adapter == float(a), ranks[a].astype(F32), rank)
    return start, adapter, rank


def kernel(
    hid, pq, pkv, down, up, ranks_h, tenant_h, lens_h, owner_h, cache, dq, dkv,
    pout, dout,
    hid_v, pq_v, pkv_v, down_v, up_v, cache_v, dkv_v, qall,
    own_num, own_st, sendb, recv_r, recv_l,
    mine, pick_v, rs_send, rs_recv, sh_own,
    kv_own, kv_oth, packed, handed, acc, acc_st, pout_v, dout_v, slot_tab,
    ranks, tenant, lens, owner,
    lsem, qs, qr, ps, pr, rss, rsr, ags, agr, xs, xr, hs, hr, osem,
):
    s = lax.axis_index("segment")
    g = lax.axis_index("group")
    t = lax.axis_index("tensor")

    loads = []
    for k, (src, dst) in enumerate(
        [(lens_h, lens), (owner_h, owner), (tenant_h, tenant), (ranks_h, ranks),
         (dq, qall.at[t]), (hid, hid_v), (down, down_v), (pkv, pkv_v), (up, up_v),
         (cache, cache_v), (dkv, dkv_v), (pq, pq_v)]
    ):
        c = pltpu.make_async_copy(src, dst, lsem.at[k])
        c.start()
        loads.append(c)
    ld_q, ld_hid, ld_down, ld_pkv, ld_up, ld_cache, ld_dkv, ld_pq = loads[4:]

    barrier = pltpu.get_barrier_semaphore()

    def greet_tensor(k, _):
        pl.semaphore_signal(barrier, inc=1, device_id={"tensor": lax.rem(t + k, NT)}, device_id_type=MESH)
        return _

    def greet_group(k, _):
        pl.semaphore_signal(barrier, inc=1, device_id={"group": lax.rem(g + k, NG)}, device_id_type=MESH)
        return _

    lax.fori_loop(1, NT, greet_tensor, 0)
    pl.semaphore_signal(barrier, inc=1, device_id={"segment": 1 - s}, device_id_type=MESH)
    lax.fori_loop(1, NG, greet_group, 0)

    for c in loads[:4]:
        c.wait()

    here = s * NG + g
    there = (1 - s) * NG + g
    lane = iota((8, 128), 1)
    tenants = jnp.zeros((8, 128), jnp.int32)
    for i in range(REQ):
        tenants = jnp.where(lane == i, tenant[0, i], tenants)
    start_row, end_row, _ = request_rows(lens, owner, here)
    start, adapter, rank = token_columns(start_row, end_row, tenants[0:1], ranks)

    ld_hid.wait()
    ld_down.wait()
    col = iota((TOK, HEAD), 1)
    selected = jnp.zeros((TOK, HEAD), F32)
    for a in range(ADAPTERS):
        part = jnp.dot(hid_v[...], down_v[a], preferred_element_type=F32)
        selected = jnp.where(adapter == float(a), part, selected)
    selected = jnp.where(col.astype(F32) < rank, selected, 0.0)
    mine[...] = selected.reshape(NT, BLK, HEAD)
    rs_send[...] = mine[...].astype(BF16)

    pl.semaphore_wait(barrier, (NT - 1) + 1 + (NG - 1))

    def q_copy(j, c, side):
        rows = pl.ds(c * QROWS, QROWS)
        return pltpu.make_async_remote_copy(
            src_ref=qall.at[j, rows],
            dst_ref=qall.at[j, rows],
            send_sem=qs.at[side, j, c],
            recv_sem=qr.at[j, c],
            device_id={"tensor": lax.rem(t + (1 if side == 0 else NT - 1), NT)},
            device_id_type=MESH,
        )

    def p_copy(j, c, side):
        rows = pl.ds(0, STATS + HEAD) if c == 0 else pl.ds(STATS + c * HEAD, HEAD)
        return pltpu.make_async_remote_copy(
            src_ref=sendb.at[j, rows],
            dst_ref=(recv_r if side == 0 else recv_l).at[j, rows],
            send_sem=ps.at[side, j, c],
            recv_sem=pr.at[side, j, c],
            device_id={"tensor": lax.rem(t + (1 if side == 0 else NT - 1), NT)},
            device_id_type=MESH,
        )

    def rs_copy(k, src):
        return pltpu.make_async_remote_copy(
            src_ref=rs_send.at[k],
            dst_ref=rs_recv.at[src],
            send_sem=rss.at[k],
            recv_sem=rsr.at[src],
            device_id={"tensor": k},
            device_id_type=MESH,
        )

    def ag_copy(k, src):
        return pltpu.make_async_remote_copy(
            src_ref=sh_own.at[src],
            dst_ref=sh_own.at[src],
            send_sem=ags.at[k],
            recv_sem=agr.at[src],
            device_id={"tensor": k},
            device_id_type=MESH,
        )

    def rows_copy(half):
        return pltpu.make_async_remote_copy(
            src_ref=kv_own.at[half],
            dst_ref=kv_oth.at[half],
            send_sem=xs.at[half],
            recv_sem=xr.at[half],
            device_id={"segment": 1 - s},
            device_id_type=MESH,
        )

    def hand_copy(half, d, src):
        return pltpu.make_async_remote_copy(
            src_ref=packed.at[half, d],
            dst_ref=handed.at[half, src],
            send_sem=hs.at[half, d],
            recv_sem=hr.at[half, src],
            device_id={"group": d},
            device_id_type=MESH,
        )

    def rs_start(k, _):
        rs_copy(lax.rem(t + k, NT), t).start()
        return _

    lax.fori_loop(1, NT, rs_start, 0)
    ld_q.wait()

    @pl.when(t < NT - 1)
    def _():
        for c in range(PARTS):
            q_copy(t, c, 0).start()

    @pl.when(t > 0)
    def _():
        for c in range(PARTS):
            q_copy(t, c, 1).start()

    def reduce_and_share():
        def add(k, total):
            src = lax.rem(t + k, NT)
            rs_copy(src, src).wait_recv()
            return total + rs_recv[src].astype(F32)

        total = lax.fori_loop(1, NT, add, mine[t])
        sh_own[t] = total.astype(BF16)

        def share(k, _):
            to = lax.rem(t + k, NT)
            ag_copy(to, t).start()
            return _

        lax.fori_loop(1, NT, share, 0)

    def lora_rows(shrunk, base, adapter_col, rank_col):
        delta = jnp.zeros((TOK, KVW), F32)
        for a in range(ADAPTERS):
            part = jnp.dot(shrunk, up_v[a], preferred_element_type=F32)
            delta = jnp.where(adapter_col == float(a), part, delta)
        return (base.astype(F32) + (8.0 / jnp.sqrt(rank_col)) * delta).astype(BF16)

    def find_rows():
        start_p, end_p, owner_p = request_rows(lens, owner, there)
        group_of = iota((NG * MAXLEN, 128), 0) // MAXLEN
        code = (start_p * 64 + (end_p - start_p)).astype(F32)
        found = jnp.sum(jnp.where(group_of == owner_p, code, 0.0), axis=1, keepdims=True)
        found = found.astype(jnp.int32)
        offset = iota((NG * MAXLEN, 1), 0) % MAXLEN
        source = jnp.where(offset < found % 64, found // 64 + offset, -1)
        pick_v[...] = (iota((NG * MAXLEN, TOK), 1) == source).astype(F32).astype(BF16)

    def hand_over(half):
        rows_copy(half).wait_recv()
        moved = jnp.dot(pick_v[...], kv_oth[half], preferred_element_type=F32).astype(BF16)
        packed[half] = moved.reshape(NG, MAXLEN, HEAD)

        def send(k, _):
            hand_copy(half, lax.rem(g + k, NG), g).start()
            return _

        lax.fori_loop(1, NG, send, 0)
        handed[half, g] = packed[half, g]

    def own_rows():
        def arrive(k, _):
            src = lax.rem(t + k, NT)
            ag_copy(src, src).wait_recv()
            return _

        lax.fori_loop(1, NT, arrive, 0)
        rows = lora_rows(sh_own[...].reshape(TOK, HEAD), pkv_v[...], adapter, rank)
        for half in range(2):
            kv_own[half] = rows[:, half * HEAD:(half + 1) * HEAD]
            rows_copy(half).start()

    def prompt_tile(n):
        low = max(n * TILE - 32, 0)
        keys = kv_own[0, low:low + 128]
        values = kv_own[1, low:low + 128]
        q_pos = iota((TILE, 128), 0) + n * TILE
        k_pos = iota((TILE, 128), 1) + low
        first = start[n * TILE:(n + 1) * TILE].astype(jnp.int32)
        mask = (k_pos >= first) & (k_pos <= q_pos)
        rows = slice(n * TILE, (n + 1) * TILE)
        q = jnp.concatenate([pq_v[rows, h * HEAD:(h + 1) * HEAD] for h in range(GQA)], axis=0)
        sc = (nt_dot(q, keys) * SCALE).reshape(GQA, TILE, 128)
        sc = jnp.where(mask[None], sc, NEG).reshape(GQA * TILE, 128)
        e = jnp.exp(sc - jnp.max(sc, axis=1, keepdims=True))
        w = (e * (1.0 / jnp.sum(e, axis=1, keepdims=True))).astype(BF16)
        o = jnp.dot(w, values, preferred_element_type=F32).astype(BF16)
        for h in range(GQA):
            pout_v[rows, h * HEAD:(h + 1) * HEAD] = o[h * TILE:(h + 1) * TILE]

    def out_copy(n):
        rows = pl.ds(n * TILE, TILE)
        return pltpu.make_async_copy(pout_v.at[rows], pout.at[rows], osem.at[n])

    q_lane = iota((128, 128), 1) % QROWS
    k_row = iota((128, 128), 0)
    same_slot = (k_row // MAXLEN) == (q_lane // SPEC)

    def stacked(j, part):
        rows = slice(part * QROWS, (part + 1) * QROWS)
        return jnp.concatenate([qall[j, rows, h * HEAD:(h + 1) * HEAD] for h in range(GQA)], axis=0)

    def cached_partial(j, part):
        at = pl.multiple_of(j * KVW, KVW)
        slots = slice(part * 4, part * 4 + 4)
        keys = cache_v[slots, :, pl.ds(at, HEAD)].reshape(128, HEAD)
        values = cache_v[slots, :, pl.ds(at + HEAD, HEAD)].reshape(128, HEAD)
        return partial_attention(keys, values, stacked(j, part), same_slot)

    def put_stats(j, stats):
        rows = []
        for m, total in stats:
            high = total.astype(BF16).astype(F32)
            rows += [m, high, total - high]
        rows.append(jnp.zeros((STATS - len(rows), 128), F32))
        sendb[j, 0:STATS, :] = jnp.concatenate(rows, axis=0).astype(BF16)

    def put_num(j, part, num):
        at = STATS + part * HEAD
        sendb[j, at:at + HEAD, :] = num.astype(BF16)

    def get_stats(buf, j):
        st = buf[j, 0:STATS, :].astype(F32)
        return [(st[3 * p:3 * p + 1], st[3 * p + 1:3 * p + 2] + st[3 * p + 2:3 * p + 3]) for p in range(PARTS)]

    def get_num(buf, j, part):
        at = STATS + part * HEAD
        return buf[j, at:at + HEAD, :].astype(F32)

    def own_partial(j, part):
        return own_num[j, part], own_st[j, part, 0:1, :], own_st[j, part, 1:2, :]

    def attend_head(j):
        for part in range(PARTS):
            num, m, total = cached_partial(j, part)
            own_num[j, part] = num
            own_st[j, part, 0:1, :] = m
            own_st[j, part, 1:2, :] = total

    def first_link(j, side):
        put_stats(j, [own_partial(j, part)[1:] for part in range(PARTS)])
        for part in range(PARTS):
            put_num(j, part, own_num[j, part])
            p_copy(j, part, side).start()

    def next_link(j, side):
        buf = recv_r if side == 0 else recv_l
        p_copy(j, 0, side).wait_recv()
        stats, factors = [], []
        for part, (m_in, total_in) in enumerate(get_stats(buf, j)):
            _, m_own, total_own = own_partial(j, part)
            m = jnp.maximum(m_in, m_own)
            f_in, f_own = jnp.exp(m_in - m), jnp.exp(m_own - m)
            stats.append((m, total_in * f_in + total_own * f_own))
            factors.append((f_in, f_own))
        put_stats(j, stats)
        for part, (f_in, f_own) in enumerate(factors):
            if part > 0:
                p_copy(j, part, side).wait_recv()
            put_num(j, part, get_num(buf, j, part) * f_in + own_num[j, part] * f_own)
            p_copy(j, part, side).start()

    def put_acc(part, num, m, total):
        acc[part] = num
        acc_st[part, 0:1, :] = m
        acc_st[part, 1:2, :] = total

    def get_acc(part):
        return acc[part], acc_st[part, 0:1, :], acc_st[part, 1:2, :]

    def own_and_drafts():
        k_draft = iota((QROWS, 128), 0)
        q_draft = iota((QROWS, 128), 1) % QROWS
        mask = (k_draft // SPEC == q_draft // SPEC) & (k_draft % SPEC <= q_draft % SPEC)
        for part in range(PARTS):
            rows = slice(part * QROWS, (part + 1) * QROWS)
            draft = partial_attention(
                dkv_v[rows, 0:HEAD], dkv_v[rows, HEAD:KVW], stacked(t, part), mask
            )
            put_acc(part, *merge(cached_partial(t, part), draft))

    def find_slots():
        other = (1 - s) * NG
        for i in range(REQ):
            def look(k, src):
                return jnp.where(owner[i, other + k] == g, k, src)

            src = lax.fori_loop(0, NG, look, jnp.int32(0), unroll=True)
            slot_tab[0, i] = src
            slot_tab[1, i] = lens[i, other + src]

    def handed_attention():
        def arrive(k, _):
            src = lax.rem(g + k, NG)
            hand_copy(0, src, src).wait_recv()
            hand_copy(1, src, src).wait_recv()
            return _

        lax.fori_loop(1, NG, arrive, 0)
        for part in range(PARTS):
            keys, values = [], []
            limit = jnp.zeros((128, 128), jnp.int32)
            for u in range(4):
                i = part * 4 + u
                keys.append(handed[0, slot_tab[0, i]])
                values.append(handed[1, slot_tab[0, i]])
                limit = jnp.where(k_row // MAXLEN == u, slot_tab[1, i], limit)
            mask = same_slot & (k_row % MAXLEN < limit)
            found = partial_attention(
                jnp.concatenate(keys, axis=0), jnp.concatenate(values, axis=0), stacked(t, part), mask
            )
            put_acc(part, *merge(get_acc(part), found))

    def finish(side):
        buf = recv_r if side == 0 else recv_l
        for part in range(PARTS):
            p_copy(t, part, side).wait_recv()
        stats = get_stats(buf, t)
        for part in range(PARTS):
            put_acc(part, *merge(get_acc(part), (get_num(buf, t, part), *stats[part])))

    def step(tau, carry):
        from_right = t + tau
        from_left = t - tau

        @pl.when(from_right < NT)
        def _():
            for c in range(PARTS):
                q_copy(from_right, c, 1).wait_recv()

                @pl.when(t > 0)
                def _():
                    q_copy(from_right, c, 1).start()

        @pl.when(from_left >= 0)
        def _():
            for c in range(PARTS):
                q_copy(from_left, c, 0).wait_recv()

                @pl.when(t < NT - 1)
                def _():
                    q_copy(from_left, c, 0).start()

        @pl.when(from_right < NT)
        def _():
            attend_head(from_right)

            @pl.when(t == 0)
            def _():
                first_link(from_right, 0)

        @pl.when(from_left >= 0)
        def _():
            attend_head(from_left)

            @pl.when(t == NT - 1)
            def _():
                first_link(from_left, 1)

        to_right = tau - t

        @pl.when((t >= 1) & (to_right > t) & (to_right < NT))
        def _():
            next_link(to_right, 0)

        to_left = 2 * (NT - 1) - t - tau

        @pl.when((t <= NT - 2) & (to_left < t) & (to_left >= 0))
        def _():
            next_link(to_left, 1)

        @pl.when(tau == SHARE_AT)
        def _():
            reduce_and_share()

        @pl.when(tau == OWN_AT)
        def _():
            own_rows()

        for half in range(2):
            @pl.when(tau == HAND_AT[half])
            def _(half=half):
                hand_over(half)

        for n in range(TOK // TILE):
            @pl.when(tau == TILE_AT[n])
            def _(n=n):
                prompt_tile(n)
                out_copy(n).start()

        @pl.when(tau == HANDED_AT)
        def _():
            handed_attention()

        return carry

    ld_cache.wait()
    ld_dkv.wait()
    ld_pkv.wait()
    ld_up.wait()
    ld_pq.wait()
    own_and_drafts()
    find_rows()
    find_slots()
    lax.fori_loop(1, 2 * NT - 1, step, 0)

    @pl.when(t > 0)
    def _():
        finish(0)

    @pl.when(t < NT - 1)
    def _():
        finish(1)

    for part in range(PARTS):
        num, _, total = get_acc(part)
        out = jnp.transpose(num / total)
        for h in range(GQA):
            dout_v[part * QROWS:(part + 1) * QROWS, h * HEAD:(h + 1) * HEAD] = out[
                h * QROWS:(h + 1) * QROWS
            ].astype(BF16)
    last = pltpu.make_async_copy(dout_v, dout, osem.at[TOK // TILE])
    last.start()

    for side in range(2):
        edge = (t < NT - 1) if side == 0 else (t > 0)

        @pl.when(edge)
        def _(side=side):
            def each(j, carry):
                @pl.when((j <= t) if side == 0 else (j >= t))
                def _():
                    for c in range(PARTS):
                        q_copy(j, c, side).wait_send()

                @pl.when((j > t) if side == 0 else (j < t))
                def _():
                    for c in range(PARTS):
                        p_copy(j, c, side).wait_send()

                return carry

            lax.fori_loop(0, NT, each, 0)

    def left_tensor(k, _):
        to = lax.rem(t + k, NT)
        rs_copy(to, t).wait_send()
        ag_copy(to, t).wait_send()
        return _

    lax.fori_loop(1, NT, left_tensor, 0)
    for half in range(2):
        rows_copy(half).wait_send()

    def left_group(k, _):
        hand_copy(0, lax.rem(g + k, NG), g).wait_send()
        hand_copy(1, lax.rem(g + k, NG), g).wait_send()
        return _

    lax.fori_loop(1, NG, left_group, 0)
    for n in range(TOK // TILE):
        out_copy(n).wait()
    last.wait()


def body(*args):
    args = list(args)
    args[7], args[8] = args[7].T, args[8].T
    hbm = pl.BlockSpec(memory_space=pltpu.HBM)
    dma = pltpu.SemaphoreType.DMA
    return pl.pallas_call(
        kernel,
        out_shape=(
            jax.ShapeDtypeStruct((TOK, GQA * HEAD), BF16),
            jax.ShapeDtypeStruct((REQ * SPEC, GQA * HEAD), BF16),
        ),
        in_specs=[hbm] * 12,
        out_specs=(hbm, hbm),
        scratch_shapes=[
            pltpu.VMEM((TOK, NT * HEAD), BF16),
            pltpu.VMEM((TOK, GQA * HEAD), BF16),
            pltpu.VMEM((TOK, KVW), BF16),
            pltpu.VMEM((ADAPTERS, NT * HEAD, HEAD), BF16),
            pltpu.VMEM((ADAPTERS, HEAD, KVW), BF16),
            pltpu.VMEM((REQ, 32, NT * KVW), BF16),
            pltpu.VMEM((REQ * SPEC, KVW), BF16),
            pltpu.VMEM((NT, REQ * SPEC, GQA * HEAD), BF16),
            pltpu.VMEM((NT, PARTS, HEAD, 128), F32),
            pltpu.VMEM((NT, PARTS, 8, 128), F32),
            pltpu.VMEM((NT, MSG, 128), BF16),
            pltpu.VMEM((NT, MSG, 128), BF16),
            pltpu.VMEM((NT, MSG, 128), BF16),
            pltpu.VMEM((NT, BLK, HEAD), F32),
            pltpu.VMEM((NG * MAXLEN, TOK), BF16),
            pltpu.VMEM((NT, BLK, HEAD), BF16),
            pltpu.VMEM((NT, BLK, HEAD), BF16),
            pltpu.VMEM((NT, BLK, HEAD), BF16),
            pltpu.VMEM((2, TOK, HEAD), BF16),
            pltpu.VMEM((2, TOK, HEAD), BF16),
            pltpu.VMEM((2, NG, MAXLEN, HEAD), BF16),
            pltpu.VMEM((2, NG, MAXLEN, HEAD), BF16),
            pltpu.VMEM((PARTS, HEAD, 128), F32),
            pltpu.VMEM((PARTS, 8, 128), F32),
            pltpu.VMEM((TOK, GQA * HEAD), BF16),
            pltpu.VMEM((REQ * SPEC, GQA * HEAD), BF16),
            pltpu.SMEM((2, REQ), jnp.int32),
            pltpu.SMEM((ADAPTERS,), jnp.int32),
            pltpu.SMEM((1, REQ), jnp.int32),
            pltpu.SMEM((REQ, 2 * NG), jnp.int32),
            pltpu.SMEM((REQ, 2 * NG), jnp.int32),
            dma((12,)),
            dma((2, NT, PARTS)),
            dma((NT, PARTS)),
            dma((2, NT, PARTS)),
            dma((2, NT, PARTS)),
            dma((NT,)),
            dma((NT,)),
            dma((NT,)),
            dma((NT,)),
            dma((2,)),
            dma((2,)),
            dma((2, NG)),
            dma((2, NG)),
            dma((TOK // TILE + 1,)),
        ],
        compiler_params=pltpu.CompilerParams(
            collective_id=0, has_side_effects=True, vmem_limit_bytes=60 << 20
        ),
    )(*args)


def solution(mesh):
    rows = ("segment", "group")
    return jax.shard_map(
        body,
        mesh=mesh,
        in_specs=(
            P(rows, "tensor"),
            P(rows, "tensor"),
            P(rows, "tensor"),
            P(None, "tensor", None),
            P(None, None, "tensor"),
            P(),
            P(rows, None),
            P(),
            P(),
            P(rows, "tensor", None),
            P(rows, "tensor"),
            P(rows, "tensor"),
        ),
        out_specs=(P(rows, "tensor"), P(rows, "tensor")),
        check_vma=False,
    )
```

```python
import jax
import jax.numpy as jnp
from jax import lax
from jax.experimental import pallas as pl
from jax.experimental.pallas import tpu as pltpu
from jax.sharding import PartitionSpec as P

HEAD = 128
GQA = 8
SPEC = 4
MAXLEN = 32
REQ = 16
NT = 8
NG = 32
TOK = 384
BLK = TOK // NT
ADAPTERS = 3
PARTS = 4
HALF = NT // 2
QROWS = REQ * SPEC // PARTS
KVW = 2 * HEAD
STATS = 16
STEPS = 11
MSG = STATS + PARTS * HEAD
TILE = 96
SCALE = HEAD**-0.5
SHARE_AT = 3
OWN_AT = 5
HAND_AT = (9, 10)
TILE_AT = (6, 7, 8, 9)
HANDED_AT = 11
NEG = -1e30
MESH = pl.DeviceIdType.MESH
F32 = jnp.float32
BF16 = jnp.bfloat16


def nt_dot(a, b):
    return lax.dot_general(a, b, (((1,), (1,)), ((), ())), preferred_element_type=F32)


def tn_dot(a, b):
    return lax.dot_general(a, b, (((0,), (0,)), ((), ())), preferred_element_type=F32)


def iota(shape, dim):
    return lax.broadcasted_iota(jnp.int32, shape, dim)


def merge(a, b):
    num_a, m_a, l_a = a
    num_b, m_b, l_b = b
    m = jnp.maximum(m_a, m_b)
    f_a = jnp.exp(m_a - m)
    f_b = jnp.exp(m_b - m)
    return num_a * f_a + num_b * f_b, m, l_a * f_a + l_b * f_b


def partial_attention(keys, values, queries, mask):
    s = nt_dot(keys, queries) * SCALE
    s = jnp.where(mask, s, NEG)
    m = jnp.max(s, axis=0, keepdims=True).astype(BF16).astype(F32)
    p = jnp.where(mask, jnp.exp(s - m), 0.0)
    total = jnp.sum(p, axis=0, keepdims=True)
    num = tn_dot(values, p.astype(BF16))
    return num, m, total


def request_rows(lens, owner, row):
    lane = iota((1, 128), 1)
    start_row = jnp.full((1, 128), 1 << 20, jnp.int32)
    end_row = jnp.full((1, 128), 1 << 20, jnp.int32)
    owner_row = jnp.full((1, 128), -1, jnp.int32)
    at = jnp.int32(0)
    for i in range(REQ):
        n = lens[i, row]
        start_row = jnp.where(lane == i, at, start_row)
        at = at + n
        end_row = jnp.where(lane == i, at, end_row)
        owner_row = jnp.where(lane == i, owner[i, row], owner_row)
    return start_row, end_row, owner_row


def token_columns(start_row, end_row, tenant_row, ranks):
    pos = iota((TOK, 128), 0)
    hit = (pos >= start_row) & (pos < end_row)
    start = jnp.sum(jnp.where(hit, start_row.astype(F32), 0.0), axis=1, keepdims=True)
    adapter = jnp.sum(jnp.where(hit, tenant_row.astype(F32), 0.0), axis=1, keepdims=True)
    rank = jnp.zeros((TOK, 1), F32)
    for a in range(ADAPTERS):
        rank = jnp.where(adapter == float(a), ranks[a].astype(F32), rank)
    return start, adapter, rank


def kernel(
    hid, pq, pkv, down, up, ranks_h, tenant_h, lens_h, owner_h, cache, dq, dkv,
    pout, dout,
    hid_v, pq_v, pkv_v, down_v, up_v, cache_v, dkv_v, qall,
    own_num, own_st, sendb, recv_r, recv_l,
    mine, pick_v, rs_send, rs_recv, sh_own,
    kv_own, kv_oth, packed, handed, acc, acc_st, pout_v, dout_v, slot_tab,
    ranks, tenant, lens, owner,
    lsem, qs, qr, ps, pr, rss, rsr, ags, agr, xs, xr, hs, hr, osem,
):
    s = lax.axis_index("segment")
    g = lax.axis_index("group")
    t = lax.axis_index("tensor")
    low = t // HALF * HALF
    place = t - low

    loads = []
    for k, (src, dst) in enumerate(
        [(lens_h, lens), (owner_h, owner), (tenant_h, tenant), (ranks_h, ranks),
         (dq, qall.at[t]), (hid, hid_v), (down, down_v), (pkv, pkv_v), (up, up_v),
         (cache, cache_v), (dkv, dkv_v), (pq, pq_v)]
    ):
        c = pltpu.make_async_copy(src, dst, lsem.at[k])
        c.start()
        loads.append(c)
    ld_q, ld_hid, ld_down, ld_pkv, ld_up, ld_cache, ld_dkv, ld_pq = loads[4:]

    barrier = pltpu.get_barrier_semaphore()

    def greet_tensor(k, _):
        pl.semaphore_signal(barrier, inc=1, device_id={"tensor": lax.rem(t + k, NT)}, device_id_type=MESH)
        return _

    def greet_group(k, _):
        pl.semaphore_signal(barrier, inc=1, device_id={"group": lax.rem(g + k, NG)}, device_id_type=MESH)
        return _

    lax.fori_loop(1, NT, greet_tensor, 0)
    pl.semaphore_signal(barrier, inc=1, device_id={"segment": 1 - s}, device_id_type=MESH)
    lax.fori_loop(1, NG, greet_group, 0)

    def q_copy(j, c, side):
        rows = pl.ds(c * QROWS, QROWS)
        return pltpu.make_async_remote_copy(
            src_ref=qall.at[j, rows],
            dst_ref=qall.at[j, rows],
            send_sem=qs.at[side, j, c],
            recv_sem=qr.at[j, c],
            device_id={"tensor": lax.rem(t + (1 if side == 0 else NT - 1), NT)},
            device_id_type=MESH,
        )

    def part_copy(j, c, side, slot, to):
        rows = pl.ds(0, STATS + HEAD) if c == 0 else pl.ds(STATS + c * HEAD, HEAD)
        return pltpu.make_async_remote_copy(
            src_ref=sendb.at[j, rows],
            dst_ref=(recv_r if side == 0 else recv_l).at[slot, rows],
            send_sem=ps.at[side, j, c],
            recv_sem=pr.at[side, slot, c],
            device_id={"tensor": to},
            device_id_type=MESH,
        )

    def p_copy(j, c, side):
        jump = t == (HALF - 1 if side == 0 else HALF)
        near = lax.rem(t + (1 if side == 0 else NT - 1), NT)
        return part_copy(j, c, side, jnp.where(jump, NT, j), jnp.where(jump, j, near))

    def p_arrived(j, c, side, slot):
        part_copy(j, c, side, slot, lax.rem(t + 1, NT)).wait_recv()

    def rs_copy(k, src):
        return pltpu.make_async_remote_copy(
            src_ref=rs_send.at[k],
            dst_ref=rs_recv.at[src],
            send_sem=rss.at[k],
            recv_sem=rsr.at[src],
            device_id={"tensor": k},
            device_id_type=MESH,
        )

    def ag_copy(k, src):
        return pltpu.make_async_remote_copy(
            src_ref=sh_own.at[src],
            dst_ref=sh_own.at[src],
            send_sem=ags.at[k],
            recv_sem=agr.at[src],
            device_id={"tensor": k},
            device_id_type=MESH,
        )

    def rows_copy(half):
        return pltpu.make_async_remote_copy(
            src_ref=kv_own.at[half],
            dst_ref=kv_oth.at[half],
            send_sem=xs.at[half],
            recv_sem=xr.at[half],
            device_id={"segment": 1 - s},
            device_id_type=MESH,
        )

    def hand_copy(half, d, src):
        return pltpu.make_async_remote_copy(
            src_ref=packed.at[half, d],
            dst_ref=handed.at[half, src],
            send_sem=hs.at[half, d],
            recv_sem=hr.at[half, src],
            device_id={"group": d},
            device_id_type=MESH,
        )

    ld_q.wait()
    pl.semaphore_wait(barrier, (NT - 1) + 1 + (NG - 1))

    @pl.when(t < NT - 1)
    def _():
        for c in range(PARTS):
            q_copy(t, c, 0).start()

    @pl.when(t > 0)
    def _():
        for c in range(PARTS):
            q_copy(t, c, 1).start()

    for c in loads[:4]:
        c.wait()

    here = s * NG + g
    there = (1 - s) * NG + g
    lane = iota((8, 128), 1)
    tenants = jnp.zeros((8, 128), jnp.int32)
    for i in range(REQ):
        tenants = jnp.where(lane == i, tenant[0, i], tenants)
    start_row, end_row, _ = request_rows(lens, owner, here)
    start, adapter, rank = token_columns(start_row, end_row, tenants[0:1], ranks)

    ld_hid.wait()
    ld_down.wait()
    col = iota((TOK, HEAD), 1)
    selected = jnp.zeros((TOK, HEAD), F32)
    for a in range(ADAPTERS):
        part = jnp.dot(hid_v[...], down_v[a], preferred_element_type=F32)
        selected = jnp.where(adapter == float(a), part, selected)
    selected = jnp.where(col.astype(F32) < rank, selected, 0.0)
    mine[...] = selected.reshape(NT, BLK, HEAD)
    rs_send[...] = mine[...].astype(BF16)

    def rs_start(k, _):
        rs_copy(lax.rem(t + k, NT), t).start()
        return _

    lax.fori_loop(1, NT, rs_start, 0)

    def reduce_and_share():
        def add(k, total):
            src = lax.rem(t + k, NT)
            rs_copy(src, src).wait_recv()
            return total + rs_recv[src].astype(F32)

        total = lax.fori_loop(1, NT, add, mine[t])
        sh_own[t] = total.astype(BF16)

        def share(k, _):
            to = lax.rem(t + k, NT)
            ag_copy(to, t).start()
            return _

        lax.fori_loop(1, NT, share, 0)

    def lora_rows(shrunk, base, adapter_col, rank_col):
        delta = jnp.zeros((TOK, KVW), F32)
        for a in range(ADAPTERS):
            part = jnp.dot(shrunk, up_v[a], preferred_element_type=F32)
            delta = jnp.where(adapter_col == float(a), part, delta)
        return (base.astype(F32) + (8.0 / jnp.sqrt(rank_col)) * delta).astype(BF16)

    def find_rows():
        start_p, end_p, owner_p = request_rows(lens, owner, there)
        group_of = iota((NG * MAXLEN, 128), 0) // MAXLEN
        code = (start_p * 64 + (end_p - start_p)).astype(F32)
        found = jnp.sum(jnp.where(group_of == owner_p, code, 0.0), axis=1, keepdims=True)
        found = found.astype(jnp.int32)
        offset = iota((NG * MAXLEN, 1), 0) % MAXLEN
        source = jnp.where(offset < found % 64, found // 64 + offset, -1)
        pick_v[...] = (iota((NG * MAXLEN, TOK), 1) == source).astype(F32).astype(BF16)

    def hand_over(half):
        rows_copy(half).wait_recv()
        moved = jnp.dot(pick_v[...], kv_oth[half], preferred_element_type=F32).astype(BF16)
        packed[half] = moved.reshape(NG, MAXLEN, HEAD)

        def send(k, _):
            hand_copy(half, lax.rem(g + k, NG), g).start()
            return _

        lax.fori_loop(1, NG, send, 0)
        handed[half, g] = packed[half, g]

    def own_rows():
        def arrive(k, _):
            src = lax.rem(t + k, NT)
            ag_copy(src, src).wait_recv()
            return _

        lax.fori_loop(1, NT, arrive, 0)
        rows = lora_rows(sh_own[...].reshape(TOK, HEAD), pkv_v[...], adapter, rank)
        for half in range(2):
            kv_own[half] = rows[:, half * HEAD:(half + 1) * HEAD]
            rows_copy(half).start()

    def prompt_tile(n):
        first_key = max(n * TILE - 32, 0)
        keys = kv_own[0, first_key:first_key + 128]
        values = kv_own[1, first_key:first_key + 128]
        q_pos = iota((TILE, 128), 0) + n * TILE
        k_pos = iota((TILE, 128), 1) + first_key
        first = start[n * TILE:(n + 1) * TILE].astype(jnp.int32)
        mask = (k_pos >= first) & (k_pos <= q_pos)
        rows = slice(n * TILE, (n + 1) * TILE)
        q = jnp.concatenate([pq_v[rows, h * HEAD:(h + 1) * HEAD] for h in range(GQA)], axis=0)
        sc = (nt_dot(q, keys) * SCALE).reshape(GQA, TILE, 128)
        sc = jnp.where(mask[None], sc, NEG).reshape(GQA * TILE, 128)
        e = jnp.exp(sc - jnp.max(sc, axis=1, keepdims=True))
        w = (e * (1.0 / jnp.sum(e, axis=1, keepdims=True))).astype(BF16)
        o = jnp.dot(w, values, preferred_element_type=F32).astype(BF16)
        for h in range(GQA):
            pout_v[rows, h * HEAD:(h + 1) * HEAD] = o[h * TILE:(h + 1) * TILE]

    def out_copy(n):
        rows = pl.ds(n * TILE, TILE)
        return pltpu.make_async_copy(pout_v.at[rows], pout.at[rows], osem.at[n])

    q_lane = iota((128, 128), 1) % QROWS
    k_row = iota((128, 128), 0)
    same_slot = (k_row // MAXLEN) == (q_lane // SPEC)

    def stacked(j, part):
        rows = slice(part * QROWS, (part + 1) * QROWS)
        return jnp.concatenate([qall[j, rows, h * HEAD:(h + 1) * HEAD] for h in range(GQA)], axis=0)

    def cached_partial(j, part):
        at = pl.multiple_of(j * KVW, KVW)
        slots = slice(part * 4, part * 4 + 4)
        keys = cache_v[slots, :, pl.ds(at, HEAD)].reshape(128, HEAD)
        values = cache_v[slots, :, pl.ds(at + HEAD, HEAD)].reshape(128, HEAD)
        return partial_attention(keys, values, stacked(j, part), same_slot)

    def put_stats(j, stats):
        rows = []
        for m, total in stats:
            high = total.astype(BF16).astype(F32)
            rows += [m, high, total - high]
        rows.append(jnp.zeros((STATS - len(rows), 128), F32))
        sendb[j, 0:STATS, :] = jnp.concatenate(rows, axis=0).astype(BF16)

    def put_num(j, part, num):
        at = STATS + part * HEAD
        sendb[j, at:at + HEAD, :] = num.astype(BF16)

    def get_stats(buf, j):
        st = buf[j, 0:STATS, :].astype(F32)
        return [(st[3 * p:3 * p + 1], st[3 * p + 1:3 * p + 2] + st[3 * p + 2:3 * p + 3]) for p in range(PARTS)]

    def get_num(buf, j, part):
        at = STATS + part * HEAD
        return buf[j, at:at + HEAD, :].astype(F32)

    def own_partial(j, part):
        return own_num[j, part], own_st[j, part, 0:1, :], own_st[j, part, 1:2, :]

    def attend_head(j):
        for part in range(PARTS):
            num, m, total = cached_partial(j, part)
            own_num[j, part] = num
            own_st[j, part, 0:1, :] = m
            own_st[j, part, 1:2, :] = total

    def first_link(j, side):
        put_stats(j, [own_partial(j, part)[1:] for part in range(PARTS)])
        for part in range(PARTS):
            put_num(j, part, own_num[j, part])
            p_copy(j, part, side).start()

    def next_link(j, side):
        buf = recv_r if side == 0 else recv_l
        p_arrived(j, 0, side, j)
        stats, factors = [], []
        for part, (m_in, total_in) in enumerate(get_stats(buf, j)):
            _, m_own, total_own = own_partial(j, part)
            m = jnp.maximum(m_in, m_own)
            f_in, f_own = jnp.exp(m_in - m), jnp.exp(m_own - m)
            stats.append((m, total_in * f_in + total_own * f_own))
            factors.append((f_in, f_own))
        put_stats(j, stats)
        for part, (f_in, f_own) in enumerate(factors):
            if part > 0:
                p_arrived(j, part, side, j)
            put_num(j, part, get_num(buf, j, part) * f_in + own_num[j, part] * f_own)
            p_copy(j, part, side).start()

    def put_acc(part, num, m, total):
        acc[part] = num
        acc_st[part, 0:1, :] = m
        acc_st[part, 1:2, :] = total

    def get_acc(part):
        return acc[part], acc_st[part, 0:1, :], acc_st[part, 1:2, :]

    def own_and_drafts():
        k_draft = iota((QROWS, 128), 0)
        q_draft = iota((QROWS, 128), 1) % QROWS
        mask = (k_draft // SPEC == q_draft // SPEC) & (k_draft % SPEC <= q_draft % SPEC)
        for part in range(PARTS):
            rows = slice(part * QROWS, (part + 1) * QROWS)
            draft = partial_attention(
                dkv_v[rows, 0:HEAD], dkv_v[rows, HEAD:KVW], stacked(t, part), mask
            )
            put_acc(part, *merge(cached_partial(t, part), draft))

    def find_slots():
        other = (1 - s) * NG
        for i in range(REQ):
            def look(k, src):
                return jnp.where(owner[i, other + k] == g, k, src)

            src = lax.fori_loop(0, NG, look, jnp.int32(0), unroll=True)
            slot_tab[0, i] = src
            slot_tab[1, i] = lens[i, other + src]

    def handed_attention():
        def arrive(k, _):
            src = lax.rem(g + k, NG)
            hand_copy(0, src, src).wait_recv()
            hand_copy(1, src, src).wait_recv()
            return _

        lax.fori_loop(1, NG, arrive, 0)
        for part in range(PARTS):
            keys, values = [], []
            limit = jnp.zeros((128, 128), jnp.int32)
            for u in range(4):
                i = part * 4 + u
                keys.append(handed[0, slot_tab[0, i]])
                values.append(handed[1, slot_tab[0, i]])
                limit = jnp.where(k_row // MAXLEN == u, slot_tab[1, i], limit)
            mask = same_slot & (k_row % MAXLEN < limit)
            found = partial_attention(
                jnp.concatenate(keys, axis=0), jnp.concatenate(values, axis=0), stacked(t, part), mask
            )
            put_acc(part, *merge(get_acc(part), found))

    def finish(side, slot):
        buf = recv_r if side == 0 else recv_l
        for part in range(PARTS):
            p_arrived(t, part, side, slot)
        stats = get_stats(buf, slot)
        for part in range(PARTS):
            put_acc(part, *merge(get_acc(part), (get_num(buf, slot, part), *stats[part])))

    def step(tau, carry):
        from_right = t + tau
        from_left = t - tau

        @pl.when(from_right < NT)
        def _():
            for c in range(PARTS):
                q_copy(from_right, c, 1).wait_recv()

                @pl.when(t > 0)
                def _():
                    q_copy(from_right, c, 1).start()

        @pl.when(from_left >= 0)
        def _():
            for c in range(PARTS):
                q_copy(from_left, c, 0).wait_recv()

                @pl.when(t < NT - 1)
                def _():
                    q_copy(from_left, c, 0).start()

        @pl.when(from_right < NT)
        def _():
            attend_head(from_right)

            @pl.when(place == 0)
            def _():
                first_link(from_right, 0)

        @pl.when(from_left >= 0)
        def _():
            attend_head(from_left)

            @pl.when(place == HALF - 1)
            def _():
                first_link(from_left, 1)

        to_right = tau - t + 2 * low

        @pl.when((place >= 1) & (to_right > t) & (to_right < NT))
        def _():
            next_link(to_right, 0)

        to_left = 2 * (low + HALF - 1) - t - tau

        @pl.when((place <= HALF - 2) & (to_left < t) & (to_left >= 0))
        def _():
            next_link(to_left, 1)

        @pl.when(tau == SHARE_AT)
        def _():
            reduce_and_share()

        @pl.when(tau == OWN_AT)
        def _():
            own_rows()

        for half in range(2):
            @pl.when(tau == HAND_AT[half])
            def _(half=half):
                hand_over(half)

        for n in range(TOK // TILE):
            @pl.when(tau == TILE_AT[n])
            def _(n=n):
                prompt_tile(n)
                out_copy(n).start()

        @pl.when(tau == HANDED_AT)
        def _():
            handed_attention()

        return carry

    ld_cache.wait()
    ld_dkv.wait()
    ld_pkv.wait()
    ld_up.wait()
    ld_pq.wait()
    own_and_drafts()
    find_rows()
    find_slots()
    lax.fori_loop(1, STEPS + 1, step, 0)

    @pl.when(place > 0)
    def _():
        finish(0, t)

    @pl.when(place < HALF - 1)
    def _():
        finish(1, t)

    @pl.when(t >= HALF)
    def _():
        finish(0, NT)

    @pl.when(t < HALF)
    def _():
        finish(1, NT)

    for part in range(PARTS):
        num, _, total = get_acc(part)
        out = jnp.transpose(num / total)
        for h in range(GQA):
            dout_v[part * QROWS:(part + 1) * QROWS, h * HEAD:(h + 1) * HEAD] = out[
                h * QROWS:(h + 1) * QROWS
            ].astype(BF16)
    last = pltpu.make_async_copy(dout_v, dout, osem.at[TOK // TILE])
    last.start()

    for side in range(2):
        edge = (t < NT - 1) if side == 0 else (t > 0)

        @pl.when(edge)
        def _(side=side):
            def each(j, carry):
                @pl.when((j <= t) if side == 0 else (j >= t))
                def _():
                    for c in range(PARTS):
                        q_copy(j, c, side).wait_send()

                @pl.when((j > t) if side == 0 else (j < t))
                def _():
                    for c in range(PARTS):
                        p_copy(j, c, side).wait_send()

                return carry

            lax.fori_loop(0, NT, each, 0)

    def left_tensor(k, _):
        to = lax.rem(t + k, NT)
        rs_copy(to, t).wait_send()
        ag_copy(to, t).wait_send()
        return _

    lax.fori_loop(1, NT, left_tensor, 0)
    for half in range(2):
        rows_copy(half).wait_send()

    def left_group(k, _):
        hand_copy(0, lax.rem(g + k, NG), g).wait_send()
        hand_copy(1, lax.rem(g + k, NG), g).wait_send()
        return _

    lax.fori_loop(1, NG, left_group, 0)
    for n in range(TOK // TILE):
        out_copy(n).wait()
    last.wait()


def body(*args):
    args = list(args)
    args[7], args[8] = args[7].T, args[8].T
    hbm = pl.BlockSpec(memory_space=pltpu.HBM)
    dma = pltpu.SemaphoreType.DMA
    return pl.pallas_call(
        kernel,
        out_shape=(
            jax.ShapeDtypeStruct((TOK, GQA * HEAD), BF16),
            jax.ShapeDtypeStruct((REQ * SPEC, GQA * HEAD), BF16),
        ),
        in_specs=[hbm] * 12,
        out_specs=(hbm, hbm),
        scratch_shapes=[
            pltpu.VMEM((TOK, NT * HEAD), BF16),
            pltpu.VMEM((TOK, GQA * HEAD), BF16),
            pltpu.VMEM((TOK, KVW), BF16),
            pltpu.VMEM((ADAPTERS, NT * HEAD, HEAD), BF16),
            pltpu.VMEM((ADAPTERS, HEAD, KVW), BF16),
            pltpu.VMEM((REQ, 32, NT * KVW), BF16),
            pltpu.VMEM((REQ * SPEC, KVW), BF16),
            pltpu.VMEM((NT, REQ * SPEC, GQA * HEAD), BF16),
            pltpu.VMEM((NT, PARTS, HEAD, 128), F32),
            pltpu.VMEM((NT, PARTS, 8, 128), F32),
            pltpu.VMEM((NT, MSG, 128), BF16),
            pltpu.VMEM((NT + 1, MSG, 128), BF16),
            pltpu.VMEM((NT + 1, MSG, 128), BF16),
            pltpu.VMEM((NT, BLK, HEAD), F32),
            pltpu.VMEM((NG * MAXLEN, TOK), BF16),
            pltpu.VMEM((NT, BLK, HEAD), BF16),
            pltpu.VMEM((NT, BLK, HEAD), BF16),
            pltpu.VMEM((NT, BLK, HEAD), BF16),
            pltpu.VMEM((2, TOK, HEAD), BF16),
            pltpu.VMEM((2, TOK, HEAD), BF16),
            pltpu.VMEM((2, NG, MAXLEN, HEAD), BF16),
            pltpu.VMEM((2, NG, MAXLEN, HEAD), BF16),
            pltpu.VMEM((PARTS, HEAD, 128), F32),
            pltpu.VMEM((PARTS, 8, 128), F32),
            pltpu.VMEM((TOK, GQA * HEAD), BF16),
            pltpu.VMEM((REQ * SPEC, GQA * HEAD), BF16),
            pltpu.SMEM((2, REQ), jnp.int32),
            pltpu.SMEM((ADAPTERS,), jnp.int32),
            pltpu.SMEM((1, REQ), jnp.int32),
            pltpu.SMEM((REQ, 2 * NG), jnp.int32),
            pltpu.SMEM((REQ, 2 * NG), jnp.int32),
            dma((12,)),
            dma((2, NT, PARTS)),
            dma((NT, PARTS)),
            dma((2, NT, PARTS)),
            dma((2, NT + 1, PARTS)),
            dma((NT,)),
            dma((NT,)),
            dma((NT,)),
            dma((NT,)),
            dma((2,)),
            dma((2,)),
            dma((2, NG)),
            dma((2, NG)),
            dma((TOK // TILE + 1,)),
        ],
        compiler_params=pltpu.CompilerParams(
            collective_id=0, has_side_effects=True, vmem_limit_bytes=60 << 20
        ),
    )(*args)


def solution(mesh):
    rows = ("segment", "group")
    return jax.shard_map(
        body,
        mesh=mesh,
        in_specs=(
            P(rows, "tensor"),
            P(rows, "tensor"),
            P(rows, "tensor"),
            P(None, "tensor", None),
            P(None, None, "tensor"),
            P(),
            P(rows, None),
            P(),
            P(),
            P(rows, "tensor", None),
            P(rows, "tensor"),
            P(rows, "tensor"),
        ),
        out_specs=(P(rows, "tensor"), P(rows, "tensor")),
        check_vma=False,
    )
```

```python
import jax
import jax.numpy as jnp
from jax import lax
from jax.experimental import pallas as pl
from jax.experimental.pallas import tpu as pltpu
from jax.sharding import PartitionSpec as P

HEAD = 128
GQA = 8
SPEC = 4
MAXLEN = 32
REQ = 16
NT = 8
NG = 32
TOK = 384
BLK = TOK // NT
ADAPTERS = 3
PARTS = 4
HALF = NT // 2
QROWS = REQ * SPEC // PARTS
KVW = 2 * HEAD
STATS = 16
STEPS = 11
MSG = STATS + PARTS * HEAD
TILE = 96
SCALE = HEAD**-0.5
SHARE_AT = 3
LOCAL_AT = (1, 2, 4)
OWN_AT = 5
HAND_AT = (9, 10)
TILE_AT = (6, 7, 8, 9)
HANDED_AT = 11
NEG = -1e30
MESH = pl.DeviceIdType.MESH
F32 = jnp.float32
BF16 = jnp.bfloat16


def nt_dot(a, b):
    return lax.dot_general(a, b, (((1,), (1,)), ((), ())), preferred_element_type=F32)


def tn_dot(a, b):
    return lax.dot_general(a, b, (((0,), (0,)), ((), ())), preferred_element_type=F32)


def iota(shape, dim):
    return lax.broadcasted_iota(jnp.int32, shape, dim)


def merge(a, b):
    num_a, m_a, l_a = a
    num_b, m_b, l_b = b
    m = jnp.maximum(m_a, m_b)
    f_a = jnp.exp(m_a - m)
    f_b = jnp.exp(m_b - m)
    return num_a * f_a + num_b * f_b, m, l_a * f_a + l_b * f_b


def partial_attention(keys, values, queries, mask):
    s = nt_dot(keys, queries) * SCALE
    s = jnp.where(mask, s, NEG)
    m = jnp.max(s, axis=0, keepdims=True).astype(BF16).astype(F32)
    p = jnp.where(mask, jnp.exp(s - m), 0.0)
    total = jnp.sum(p, axis=0, keepdims=True)
    num = tn_dot(values, p.astype(BF16))
    return num, m, total


def request_rows(lens, owner, row):
    lane = iota((1, 128), 1)
    start_row = jnp.full((1, 128), 1 << 20, jnp.int32)
    end_row = jnp.full((1, 128), 1 << 20, jnp.int32)
    owner_row = jnp.full((1, 128), -1, jnp.int32)
    at = jnp.int32(0)
    for i in range(REQ):
        n = lens[i, row]
        start_row = jnp.where(lane == i, at, start_row)
        at = at + n
        end_row = jnp.where(lane == i, at, end_row)
        owner_row = jnp.where(lane == i, owner[i, row], owner_row)
    return start_row, end_row, owner_row


def token_columns(start_row, end_row, tenant_row, ranks):
    pos = iota((TOK, 128), 0)
    hit = (pos >= start_row) & (pos < end_row)
    start = jnp.sum(jnp.where(hit, start_row.astype(F32), 0.0), axis=1, keepdims=True)
    adapter = jnp.sum(jnp.where(hit, tenant_row.astype(F32), 0.0), axis=1, keepdims=True)
    rank = jnp.zeros((TOK, 1), F32)
    for a in range(ADAPTERS):
        rank = jnp.where(adapter == float(a), ranks[a].astype(F32), rank)
    return start, adapter, rank


def kernel(
    hid, pq, pkv, down, up, ranks_h, tenant_h, lens_h, owner_h, cache, dq, dkv,
    pout, dout,
    hid_v, pq_v, pkv_v, down_v, up_v, cache_v, dkv_v, qall,
    own_num, own_st, sendb, recv_r, recv_l,
    mine, pick_v, rs_send, rs_recv, sh_own,
    kv_own, kv_oth, packed, handed, acc, acc_st, pout_v, dout_v, slot_tab,
    ranks, tenant, lens, owner,
    lsem, qs, qr, ps, pr, rss, rsr, ags, agr, xs, xr, hs, hr, osem,
):
    s = lax.axis_index("segment")
    g = lax.axis_index("group")
    t = lax.axis_index("tensor")
    low = t // HALF * HALF
    place = t - low

    loads = []
    for k, (src, dst) in enumerate(
        [(lens_h, lens), (owner_h, owner), (tenant_h, tenant), (ranks_h, ranks),
         (dq, qall.at[t]), (hid, hid_v), (down, down_v), (pkv, pkv_v), (up, up_v),
         (cache, cache_v), (dkv, dkv_v), (pq, pq_v)]
    ):
        c = pltpu.make_async_copy(src, dst, lsem.at[k])
        c.start()
        loads.append(c)
    ld_q, ld_hid, ld_down, ld_pkv, ld_up, ld_cache, ld_dkv, ld_pq = loads[4:]

    barrier = pltpu.get_barrier_semaphore()

    def greet_tensor(k, _):
        pl.semaphore_signal(barrier, inc=1, device_id={"tensor": lax.rem(t + k, NT)}, device_id_type=MESH)
        return _

    def greet_group(k, _):
        pl.semaphore_signal(barrier, inc=1, device_id={"group": lax.rem(g + k, NG)}, device_id_type=MESH)
        return _

    lax.fori_loop(1, NT, greet_tensor, 0)
    pl.semaphore_signal(barrier, inc=1, device_id={"segment": 1 - s}, device_id_type=MESH)
    lax.fori_loop(1, NG, greet_group, 0)

    def q_copy(j, c, side):
        rows = pl.ds(c * QROWS, QROWS)
        return pltpu.make_async_remote_copy(
            src_ref=qall.at[j, rows],
            dst_ref=qall.at[j, rows],
            send_sem=qs.at[side, j, c],
            recv_sem=qr.at[j, c],
            device_id={"tensor": lax.rem(t + (1 if side == 0 else NT - 1), NT)},
            device_id_type=MESH,
        )

    def part_copy(j, c, side, slot, to):
        rows = pl.ds(0, STATS + HEAD) if c == 0 else pl.ds(STATS + c * HEAD, HEAD)
        return pltpu.make_async_remote_copy(
            src_ref=sendb.at[j, rows],
            dst_ref=(recv_r if side == 0 else recv_l).at[slot, rows],
            send_sem=ps.at[side, j, c],
            recv_sem=pr.at[side, slot, c],
            device_id={"tensor": to},
            device_id_type=MESH,
        )

    def p_copy(j, c, side):
        jump = t == (HALF - 1 if side == 0 else HALF)
        near = lax.rem(t + (1 if side == 0 else NT - 1), NT)
        return part_copy(j, c, side, jnp.where(jump, NT, j), jnp.where(jump, j, near))

    def p_arrived(j, c, side, slot):
        part_copy(j, c, side, slot, lax.rem(t + 1, NT)).wait_recv()

    def rs_copy(k, src):
        return pltpu.make_async_remote_copy(
            src_ref=rs_send.at[k],
            dst_ref=rs_recv.at[src],
            send_sem=rss.at[k],
            recv_sem=rsr.at[src],
            device_id={"tensor": k},
            device_id_type=MESH,
        )

    def ag_copy(k, src):
        return pltpu.make_async_remote_copy(
            src_ref=sh_own.at[src],
            dst_ref=sh_own.at[src],
            send_sem=ags.at[k],
            recv_sem=agr.at[src],
            device_id={"tensor": k},
            device_id_type=MESH,
        )

    def rows_copy(half):
        return pltpu.make_async_remote_copy(
            src_ref=kv_own.at[half],
            dst_ref=kv_oth.at[half],
            send_sem=xs.at[half],
            recv_sem=xr.at[half],
            device_id={"segment": 1 - s},
            device_id_type=MESH,
        )

    def hand_copy(half, d, src):
        return pltpu.make_async_remote_copy(
            src_ref=packed.at[half, d],
            dst_ref=handed.at[half, src],
            send_sem=hs.at[half, d],
            recv_sem=hr.at[half, src],
            device_id={"group": d},
            device_id_type=MESH,
        )

    ld_q.wait()
    pl.semaphore_wait(barrier, (NT - 1) + 1 + (NG - 1))

    @pl.when(t < NT - 1)
    def _():
        for c in range(PARTS):
            q_copy(t, c, 0).start()

    @pl.when(t > 0)
    def _():
        for c in range(PARTS):
            q_copy(t, c, 1).start()

    for c in loads[:4]:
        c.wait()

    here = s * NG + g
    there = (1 - s) * NG + g
    lane = iota((8, 128), 1)
    tenants = jnp.zeros((8, 128), jnp.int32)
    for i in range(REQ):
        tenants = jnp.where(lane == i, tenant[0, i], tenants)
    start_row, end_row, _ = request_rows(lens, owner, here)
    start, adapter, rank = token_columns(start_row, end_row, tenants[0:1], ranks)

    ld_hid.wait()
    ld_down.wait()
    col = iota((TOK, HEAD), 1)
    selected = jnp.zeros((TOK, HEAD), F32)
    for a in range(ADAPTERS):
        part = jnp.dot(hid_v[...], down_v[a], preferred_element_type=F32)
        selected = jnp.where(adapter == float(a), part, selected)
    selected = jnp.where(col.astype(F32) < rank, selected, 0.0)
    mine[...] = selected.reshape(NT, BLK, HEAD)
    rs_send[...] = mine[...].astype(BF16)

    def rs_start(k, _):
        rs_copy(lax.rem(t + k, NT), t).start()
        return _

    lax.fori_loop(1, NT, rs_start, 0)

    def reduce_and_share():
        def add(k, total):
            src = lax.rem(t + k, NT)
            rs_copy(src, src).wait_recv()
            return total + rs_recv[src].astype(F32)

        total = lax.fori_loop(1, NT, add, mine[t])
        sh_own[t] = total.astype(BF16)

        def share(k, _):
            to = lax.rem(t + k, NT)
            ag_copy(to, t).start()
            return _

        lax.fori_loop(1, NT, share, 0)

    def lora_rows(shrunk, base, adapter_col, rank_col):
        delta = jnp.zeros((TOK, KVW), F32)
        for a in range(ADAPTERS):
            part = jnp.dot(shrunk, up_v[a], preferred_element_type=F32)
            delta = jnp.where(adapter_col == float(a), part, delta)
        return (base.astype(F32) + (8.0 / jnp.sqrt(rank_col)) * delta).astype(BF16)

    def find_rows():
        start_p, end_p, owner_p = request_rows(lens, owner, there)
        group_of = iota((NG * MAXLEN, 128), 0) // MAXLEN
        code = (start_p * 64 + (end_p - start_p)).astype(F32)
        found = jnp.sum(jnp.where(group_of == owner_p, code, 0.0), axis=1, keepdims=True)
        found = found.astype(jnp.int32)
        offset = iota((NG * MAXLEN, 1), 0) % MAXLEN
        source = jnp.where(offset < found % 64, found // 64 + offset, -1)
        pick_v[...] = (iota((NG * MAXLEN, TOK), 1) == source).astype(F32).astype(BF16)

    def hand_over(half):
        rows_copy(half).wait_recv()
        moved = jnp.dot(pick_v[...], kv_oth[half], preferred_element_type=F32).astype(BF16)
        packed[half] = moved.reshape(NG, MAXLEN, HEAD)

        def send(k, _):
            hand_copy(half, lax.rem(g + k, NG), g).start()
            return _

        lax.fori_loop(1, NG, send, 0)
        handed[half, g] = packed[half, g]

    def own_rows():
        def arrive(k, _):
            src = lax.rem(t + k, NT)
            ag_copy(src, src).wait_recv()
            return _

        lax.fori_loop(1, NT, arrive, 0)
        rows = lora_rows(sh_own[...].reshape(TOK, HEAD), pkv_v[...], adapter, rank)
        for half in range(2):
            kv_own[half] = rows[:, half * HEAD:(half + 1) * HEAD]
            rows_copy(half).start()

    def prompt_tile(n):
        first_key = max(n * TILE - 32, 0)
        keys = kv_own[0, first_key:first_key + 128]
        values = kv_own[1, first_key:first_key + 128]
        q_pos = iota((TILE, 128), 0) + n * TILE
        k_pos = iota((TILE, 128), 1) + first_key
        first = start[n * TILE:(n + 1) * TILE].astype(jnp.int32)
        mask = (k_pos >= first) & (k_pos <= q_pos)
        rows = slice(n * TILE, (n + 1) * TILE)
        q = jnp.concatenate([pq_v[rows, h * HEAD:(h + 1) * HEAD] for h in range(GQA)], axis=0)
        sc = (nt_dot(q, keys) * SCALE).reshape(GQA, TILE, 128)
        sc = jnp.where(mask[None], sc, NEG).reshape(GQA * TILE, 128)
        e = jnp.exp(sc - jnp.max(sc, axis=1, keepdims=True))
        w = (e * (1.0 / jnp.sum(e, axis=1, keepdims=True))).astype(BF16)
        o = jnp.dot(w, values, preferred_element_type=F32).astype(BF16)
        for h in range(GQA):
            pout_v[rows, h * HEAD:(h + 1) * HEAD] = o[h * TILE:(h + 1) * TILE]

    def out_copy(n):
        rows = pl.ds(n * TILE, TILE)
        return pltpu.make_async_copy(pout_v.at[rows], pout.at[rows], osem.at[n])

    q_lane = iota((128, 128), 1) % QROWS
    k_row = iota((128, 128), 0)
    same_slot = (k_row // MAXLEN) == (q_lane // SPEC)

    def stacked(j, part):
        rows = slice(part * QROWS, (part + 1) * QROWS)
        return jnp.concatenate([qall[j, rows, h * HEAD:(h + 1) * HEAD] for h in range(GQA)], axis=0)

    def cached_partial(j, part):
        at = pl.multiple_of(j * KVW, KVW)
        slots = slice(part * 4, part * 4 + 4)
        keys = cache_v[slots, :, pl.ds(at, HEAD)].reshape(128, HEAD)
        values = cache_v[slots, :, pl.ds(at + HEAD, HEAD)].reshape(128, HEAD)
        return partial_attention(keys, values, stacked(j, part), same_slot)

    def put_stats(j, stats):
        rows = []
        for m, total in stats:
            high = total.astype(BF16).astype(F32)
            rows += [m, high, total - high]
        rows.append(jnp.zeros((STATS - len(rows), 128), F32))
        sendb[j, 0:STATS, :] = jnp.concatenate(rows, axis=0).astype(BF16)

    def put_num(j, part, num):
        at = STATS + part * HEAD
        sendb[j, at:at + HEAD, :] = num.astype(BF16)

    def get_stats(buf, j):
        st = buf[j, 0:STATS, :].astype(F32)
        return [(st[3 * p:3 * p + 1], st[3 * p + 1:3 * p + 2] + st[3 * p + 2:3 * p + 3]) for p in range(PARTS)]

    def get_num(buf, j, part):
        at = STATS + part * HEAD
        return buf[j, at:at + HEAD, :].astype(F32)

    def own_partial(j, part):
        return own_num[j, part], own_st[j, part, 0:1, :], own_st[j, part, 1:2, :]

    def attend_head(j):
        for part in range(PARTS):
            num, m, total = cached_partial(j, part)
            own_num[j, part] = num
            own_st[j, part, 0:1, :] = m
            own_st[j, part, 1:2, :] = total

    def first_link(j, side):
        put_stats(j, [own_partial(j, part)[1:] for part in range(PARTS)])
        for part in range(PARTS):
            put_num(j, part, own_num[j, part])
            p_copy(j, part, side).start()

    def next_link(j, side):
        buf = recv_r if side == 0 else recv_l
        p_arrived(j, 0, side, j)
        stats, factors = [], []
        for part, (m_in, total_in) in enumerate(get_stats(buf, j)):
            _, m_own, total_own = own_partial(j, part)
            m = jnp.maximum(m_in, m_own)
            f_in, f_own = jnp.exp(m_in - m), jnp.exp(m_own - m)
            stats.append((m, total_in * f_in + total_own * f_own))
            factors.append((f_in, f_own))
        put_stats(j, stats)
        for part, (f_in, f_own) in enumerate(factors):
            if part > 0:
                p_arrived(j, part, side, j)
            put_num(j, part, get_num(buf, j, part) * f_in + own_num[j, part] * f_own)
            p_copy(j, part, side).start()

    def put_acc(part, num, m, total):
        acc[part] = num
        acc_st[part, 0:1, :] = m
        acc_st[part, 1:2, :] = total

    def get_acc(part):
        return acc[part], acc_st[part, 0:1, :], acc_st[part, 1:2, :]

    def own_and_drafts():
        k_draft = iota((QROWS, 128), 0)
        q_draft = iota((QROWS, 128), 1) % QROWS
        mask = (k_draft // SPEC == q_draft // SPEC) & (k_draft % SPEC <= q_draft % SPEC)
        for part in range(PARTS):
            rows = slice(part * QROWS, (part + 1) * QROWS)
            draft = partial_attention(
                dkv_v[rows, 0:HEAD], dkv_v[rows, HEAD:KVW], stacked(t, part), mask
            )
            put_acc(part, *merge(cached_partial(t, part), draft))

    def find_slots():
        other = (1 - s) * NG
        for i in range(REQ):
            def look(k, src):
                return jnp.where(owner[i, other + k] == g, k, src)

            src = lax.fori_loop(0, NG, look, jnp.int32(0), unroll=True)
            slot_tab[0, i] = src
            slot_tab[1, i] = lens[i, other + src]

    def handed_attention():
        def arrive(k, _):
            src = lax.rem(g + k, NG)
            hand_copy(0, src, src).wait_recv()
            hand_copy(1, src, src).wait_recv()
            return _

        lax.fori_loop(1, NG, arrive, 0)
        for part in range(PARTS):
            keys, values = [], []
            limit = jnp.zeros((128, 128), jnp.int32)
            for u in range(4):
                i = part * 4 + u
                keys.append(handed[0, slot_tab[0, i]])
                values.append(handed[1, slot_tab[0, i]])
                limit = jnp.where(k_row // MAXLEN == u, slot_tab[1, i], limit)
            mask = same_slot & (k_row % MAXLEN < limit)
            found = partial_attention(
                jnp.concatenate(keys, axis=0), jnp.concatenate(values, axis=0), stacked(t, part), mask
            )
            put_acc(part, *merge(get_acc(part), found))

    def finish(side, slot):
        buf = recv_r if side == 0 else recv_l
        for part in range(PARTS):
            p_arrived(t, part, side, slot)
        stats = get_stats(buf, slot)
        for part in range(PARTS):
            put_acc(part, *merge(get_acc(part), (get_num(buf, slot, part), *stats[part])))

    def step(tau, carry):
        from_right = t + tau
        from_left = t - tau

        @pl.when(from_right < NT)
        def _():
            for c in range(PARTS):
                q_copy(from_right, c, 1).wait_recv()

                @pl.when(t > 0)
                def _():
                    q_copy(from_right, c, 1).start()

        @pl.when(from_left >= 0)
        def _():
            for c in range(PARTS):
                q_copy(from_left, c, 0).wait_recv()

                @pl.when(t < NT - 1)
                def _():
                    q_copy(from_left, c, 0).start()

        @pl.when(from_right < NT)
        def _():
            attend_head(from_right)

            @pl.when(place == 0)
            def _():
                first_link(from_right, 0)

        @pl.when(from_left >= 0)
        def _():
            attend_head(from_left)

            @pl.when(place == HALF - 1)
            def _():
                first_link(from_left, 1)

        to_right = tau - t + 2 * low

        @pl.when((place >= 1) & (to_right > t) & (to_right < NT))
        def _():
            next_link(to_right, 0)

        to_left = 2 * (low + HALF - 1) - t - tau

        @pl.when((place <= HALF - 2) & (to_left < t) & (to_left >= 0))
        def _():
            next_link(to_left, 1)

        for n, work in enumerate((find_rows, own_and_drafts, find_slots)):
            @pl.when(tau == LOCAL_AT[n])
            def _(work=work):
                work()

        @pl.when(tau == SHARE_AT)
        def _():
            reduce_and_share()

        @pl.when(tau == OWN_AT)
        def _():
            own_rows()

        for half in range(2):
            @pl.when(tau == HAND_AT[half])
            def _(half=half):
                hand_over(half)

        for n in range(TOK // TILE):
            @pl.when(tau == TILE_AT[n])
            def _(n=n):
                prompt_tile(n)
                out_copy(n).start()

        @pl.when(tau == HANDED_AT)
        def _():
            handed_attention()

        return carry

    ld_cache.wait()
    ld_dkv.wait()
    ld_pkv.wait()
    ld_up.wait()
    ld_pq.wait()
    lax.fori_loop(1, STEPS + 1, step, 0)

    @pl.when(place > 0)
    def _():
        finish(0, t)

    @pl.when(place < HALF - 1)
    def _():
        finish(1, t)

    @pl.when(t >= HALF)
    def _():
        finish(0, NT)

    @pl.when(t < HALF)
    def _():
        finish(1, NT)

    for part in range(PARTS):
        num, _, total = get_acc(part)
        out = jnp.transpose(num / total)
        for h in range(GQA):
            dout_v[part * QROWS:(part + 1) * QROWS, h * HEAD:(h + 1) * HEAD] = out[
                h * QROWS:(h + 1) * QROWS
            ].astype(BF16)
    last = pltpu.make_async_copy(dout_v, dout, osem.at[TOK // TILE])
    last.start()

    for side in range(2):
        edge = (t < NT - 1) if side == 0 else (t > 0)

        @pl.when(edge)
        def _(side=side):
            def each(j, carry):
                @pl.when((j <= t) if side == 0 else (j >= t))
                def _():
                    for c in range(PARTS):
                        q_copy(j, c, side).wait_send()

                @pl.when((j > t) if side == 0 else (j < t))
                def _():
                    for c in range(PARTS):
                        p_copy(j, c, side).wait_send()

                return carry

            lax.fori_loop(0, NT, each, 0)

    def left_tensor(k, _):
        to = lax.rem(t + k, NT)
        rs_copy(to, t).wait_send()
        ag_copy(to, t).wait_send()
        return _

    lax.fori_loop(1, NT, left_tensor, 0)
    for half in range(2):
        rows_copy(half).wait_send()

    def left_group(k, _):
        hand_copy(0, lax.rem(g + k, NG), g).wait_send()
        hand_copy(1, lax.rem(g + k, NG), g).wait_send()
        return _

    lax.fori_loop(1, NG, left_group, 0)
    for n in range(TOK // TILE):
        out_copy(n).wait()
    last.wait()


def body(*args):
    args = list(args)
    args[7], args[8] = args[7].T, args[8].T
    hbm = pl.BlockSpec(memory_space=pltpu.HBM)
    dma = pltpu.SemaphoreType.DMA
    return pl.pallas_call(
        kernel,
        out_shape=(
            jax.ShapeDtypeStruct((TOK, GQA * HEAD), BF16),
            jax.ShapeDtypeStruct((REQ * SPEC, GQA * HEAD), BF16),
        ),
        in_specs=[hbm] * 12,
        out_specs=(hbm, hbm),
        scratch_shapes=[
            pltpu.VMEM((TOK, NT * HEAD), BF16),
            pltpu.VMEM((TOK, GQA * HEAD), BF16),
            pltpu.VMEM((TOK, KVW), BF16),
            pltpu.VMEM((ADAPTERS, NT * HEAD, HEAD), BF16),
            pltpu.VMEM((ADAPTERS, HEAD, KVW), BF16),
            pltpu.VMEM((REQ, 32, NT * KVW), BF16),
            pltpu.VMEM((REQ * SPEC, KVW), BF16),
            pltpu.VMEM((NT, REQ * SPEC, GQA * HEAD), BF16),
            pltpu.VMEM((NT, PARTS, HEAD, 128), F32),
            pltpu.VMEM((NT, PARTS, 8, 128), F32),
            pltpu.VMEM((NT, MSG, 128), BF16),
            pltpu.VMEM((NT + 1, MSG, 128), BF16),
            pltpu.VMEM((NT + 1, MSG, 128), BF16),
            pltpu.VMEM((NT, BLK, HEAD), F32),
            pltpu.VMEM((NG * MAXLEN, TOK), BF16),
            pltpu.VMEM((NT, BLK, HEAD), BF16),
            pltpu.VMEM((NT, BLK, HEAD), BF16),
            pltpu.VMEM((NT, BLK, HEAD), BF16),
            pltpu.VMEM((2, TOK, HEAD), BF16),
            pltpu.VMEM((2, TOK, HEAD), BF16),
            pltpu.VMEM((2, NG, MAXLEN, HEAD), BF16),
            pltpu.VMEM((2, NG, MAXLEN, HEAD), BF16),
            pltpu.VMEM((PARTS, HEAD, 128), F32),
            pltpu.VMEM((PARTS, 8, 128), F32),
            pltpu.VMEM((TOK, GQA * HEAD), BF16),
            pltpu.VMEM((REQ * SPEC, GQA * HEAD), BF16),
            pltpu.SMEM((2, REQ), jnp.int32),
            pltpu.SMEM((ADAPTERS,), jnp.int32),
            pltpu.SMEM((1, REQ), jnp.int32),
            pltpu.SMEM((REQ, 2 * NG), jnp.int32),
            pltpu.SMEM((REQ, 2 * NG), jnp.int32),
            dma((12,)),
            dma((2, NT, PARTS)),
            dma((NT, PARTS)),
            dma((2, NT, PARTS)),
            dma((2, NT + 1, PARTS)),
            dma((NT,)),
            dma((NT,)),
            dma((NT,)),
            dma((NT,)),
            dma((2,)),
            dma((2,)),
            dma((2, NG)),
            dma((2, NG)),
            dma((TOK // TILE + 1,)),
        ],
        compiler_params=pltpu.CompilerParams(
            collective_id=0, has_side_effects=True, vmem_limit_bytes=60 << 20
        ),
    )(*args)


def solution(mesh):
    rows = ("segment", "group")
    return jax.shard_map(
        body,
        mesh=mesh,
        in_specs=(
            P(rows, "tensor"),
            P(rows, "tensor"),
            P(rows, "tensor"),
            P(None, "tensor", None),
            P(None, None, "tensor"),
            P(),
            P(rows, None),
            P(),
            P(),
            P(rows, "tensor", None),
            P(rows, "tensor"),
            P(rows, "tensor"),
        ),
        out_specs=(P(rows, "tensor"), P(rows, "tensor")),
        check_vma=False,
    )
```
